128 devices in a mesh: gx: 4 (over y), gy: 4 (over z), gz: 8 (over x, core).
Axes of the slice: x: 4, y: 4, z: 4, core: 2. Of those that a mesh axis runs over, the one named last changes fastest.
Arguments:
- positions: float32 [3, 1048576], P(None, ('gx', 'gy', 'gz')), may hold values from 0 to 1
- velocities: float32 [3, 1048576], P(None, ('gx', 'gy', 'gz')), may hold values from -6 to 6
- masses: float32 [1048576], P(('gx', 'gy', 'gz')), may hold values from 0.004 to 0.016
- time_bins: int32 [1048576], P(('gx', 'gy', 'gz')), may hold values from 0 to 3
- pair_owner: int32 [2, 16384, 2], P(None, ('gx', 'gy', 'gz')), may hold values from 0 to 127, all different within a row; in each aligned block of 128 rows (0 to 127, 128 to 255, ..., all dimensions but the last counted through in order) at most 4 rows name the same one
- pair_slot: int32 [2, 16384, 2], P(None, ('gx', 'gy', 'gz')), may hold values from 0 to 63
- local_pairs: int32 [2, 8192, 2], P(None, ('gx', 'gy', 'gz')), may hold values from 0 to 63
Outputs:
- new_positions: float32 [3, 1048576], P(None, ('gx', 'gy', 'gz'))
- new_velocities: float32 [3, 1048576], P(None, ('gx', 'gy', 'gz'))
- accel: float32 [3, 1048576], P(None, ('gx', 'gy', 'gz'))
The draws below stay inside these ranges and needn't reach their ends.
Inputs may be any that keep to these rules, and one draw needn't show every extreme that they name: `pair_owner`: each row names two different owners. Within the 128 rows of one device in one subcycle no owner is named more than 4 times, and some owner reaches exactly 4. `local_pairs`: A row may name the same leaf twice.
All inputs are finite; a program needn't handle non-finite values.
Results may differ from the reference program's by a relative error of at most 0.0003.
Values sent between devices are 32-bit elements; how exact they have to be, the bound alone decides.
No kernel may reach another device: no remote copies, remote signals or barrier semaphores. Data moves between devices by JAX's collectives and lax.ppermute only.
A program may use at most 64 MiB of HBM per device.

```python
import math
import jax
import jax.numpy as jnp
import numpy as np
from jax import lax

LEAF = 128
L_DEV = 64
PAIRS_DEV = 128
LOCAL_DEV = 64
CAP = 4
NLEAF = 8192
NPART = 1048576
REMOTE = 16384
LOCALS = 8192
DEVICES = 128


def draw_positions(key, part):
    key = jax.random.fold_in(key, 11)
    centre_key = jax.random.fold_in(key, 1)
    spread_key = jax.random.fold_in(key, 2)
    centres = 0.05 * jax.random.truncated_normal(centre_key, -3.0, 3.0, (3, NLEAF, 1), jnp.float32)
    spread = 0.07 * jax.random.truncated_normal(spread_key, -4.0, 4.0, (3, NLEAF, LEAF), jnp.float32)
    placed = 0.5 + centres + spread
    return placed.reshape(3, NLEAF * LEAF)


def plant(result, stream_key, smallest, top_value):
    longest = result.shape.index(max(result.shape))
    spots = []
    for shift in (0, 1):
        where = [jax.random.randint(jax.random.fold_in(stream_key, axis), (), 0, length) for axis, length in enumerate(result.shape)]
        where[longest] = (where[longest] + shift) % result.shape[longest]
        spots.append(tuple(where))
    return result.at[spots[0]].set(smallest).at[spots[1]].set(top_value)


def block_scale(own_key, dims, split, least, high):
    def one(axis_at, shards_of):
        heights = jax.random.uniform(jax.random.fold_in(jax.random.fold_in(own_key, 6), axis_at), (shards_of,), jnp.float32, least / len(split), high / len(split))
        return jnp.repeat(jnp.exp(heights), dims[axis_at] // shards_of).reshape((-1,) + (1,) * (len(dims) - axis_at - 1))

    loudness = one(*split[0])
    for cut in split[1:]:
        loudness = loudness * one(*cut)
    return loudness


def deal_out(key, own, number, rows, count, top, most, lean):
    ranking = jax.random.permutation(key, count)
    packed, ordinary = load_shares(count, rows * top, most, lean, True), load_shares(count, rows * top, most, lean, False)
    places = jnp.arange(count)

    def named(lengths, turn):
        used = int((lengths > 0).sum())
        fixed = max(1, used // 4)
        passed = fixed + (places - fixed + turn * (used - fixed)) % max(1, count - fixed)
        return jnp.zeros((count,), jnp.int32).at[ranking[jnp.where(places < fixed, places, passed)]].set(jnp.asarray(lengths, jnp.int32))

    lengths = jnp.where(number % 4 == 0, named(packed, number // 4), named(ordinary, number - number // 4 - 1))
    mixed = jax.random.permutation(jax.random.fold_in(own, 3), count)
    giver, receiver = mixed[0:count // 2 * 2:2], mixed[1:count // 2 * 2:2]
    margin = jnp.minimum(lengths[giver] - 1, most - lengths[receiver]) // 2
    margin = jnp.where((giver == ranking[0]) | (receiver == ranking[0]) | (lengths[receiver] == 0), 0, jnp.maximum(margin, 0))
    passed = jax.random.randint(jax.random.fold_in(own, 4), (count // 2,), 0, 1 << 20) % (margin + 1)
    lengths = lengths.at[giver].add(-passed).at[receiver].add(passed)
    items = jnp.searchsorted(jnp.cumsum(lengths), jnp.arange(rows * top), side="right").astype(jnp.int32)
    table = items.reshape(top, rows).T
    table = table[jax.random.permutation(jax.random.fold_in(own, 1), rows)]
    turn = jax.random.randint(jax.random.fold_in(own, 2), (rows, 1), 0, top)
    return jnp.take_along_axis(table, (jnp.arange(top)[None, :] + turn) % top, axis=1)


def load_shares(amount, total, limit, skew, full):
    weights = [(1 << 20) // math.isqrt(grade ** skew) + 1 for grade in range(1, amount + 1)]
    largest = limit if full else min(limit, max(-(-total // amount), total * weights[0] // sum(weights)))
    least = 1 if total - largest >= amount - 1 else 0
    given, spare = [largest] + [least] * (amount - 1), total - largest - least * (amount - 1)
    while spare > 0:
        movable = [i for i in range(1, amount) if given[i] < largest] or [i for i in range(1, amount) if given[i] < limit]
        whole, budget = sum([weights[i] for i in movable]), spare
        for i in movable:
            more = min(limit - given[i], max(1, budget * weights[i] // whole), spare)
            given[i] = given[i] + more
            spare = spare - more
    return np.array(given)


def centred(stream_key, shape, scale, most, pieces=(), kind=jnp.bfloat16):
    array = scale * jax.random.normal(stream_key, shape, jnp.float32)
    if pieces:
        array = array * block_scale(stream_key, shape, pieces, -0.22, 0.18)
    return jnp.clip(array, -most, most).astype(kind)


def setup_inputs(seed: int = 0) -> dict:
    streams_of = jax.random.split(jax.random.key(seed), 8)
    positions = draw_positions(jax.random.fold_in(streams_of[7], 71), 0)
    velocities = centred(streams_of[1], (3, NPART), 1.0, 6.0, ((1, 128),), jnp.float32)
    masses = jnp.clip(jnp.exp(math.log(0.016) - 1.3862944 * jax.random.uniform(streams_of[2], (NPART,), jnp.float32) ** block_scale(streams_of[2], (NPART,), ((0, 128),), -0.2, 0.2)), 0.004, 0.016)
    time_bins = plant(jax.random.randint(streams_of[3], (NPART,), 0, 4), jax.random.fold_in(streams_of[3], 1), 0, 3).astype(jnp.int32)
    pair_owner_keys = jax.random.split(jax.random.fold_in(streams_of[4], 1), 2 * REMOTE // PAIRS_DEV)
    pair_owner_turns = jax.random.permutation(jax.random.fold_in(streams_of[4], 3), 2 * REMOTE // PAIRS_DEV)
    pair_owner = jax.vmap(lambda own, number: deal_out(jax.random.fold_in(streams_of[4], 2), own, number, PAIRS_DEV, DEVICES, 2, CAP, 2))(pair_owner_keys, pair_owner_turns).reshape((2, REMOTE, 2))
    pair_slot = plant(jax.random.randint(streams_of[5], (2, REMOTE, 2), 0, L_DEV), jax.random.fold_in(streams_of[5], 1), 0, L_DEV - 1).astype(jnp.int32)
    local_pairs = plant(jax.random.randint(streams_of[6], (2, LOCALS, 2), 0, L_DEV), jax.random.fold_in(streams_of[6], 1), 0, L_DEV - 1).astype(jnp.int32)
    return dict(positions=positions, velocities=velocities, masses=masses, time_bins=time_bins, pair_owner=pair_owner, pair_slot=pair_slot, local_pairs=local_pairs)


SOFTENING = 0.01
CUTOFF_SQ = 0.04
TIME_STEP = 0.05

def pair_forces(left_leaf, right_leaf):
    offset = right_leaf[:, :3, None, :] - left_leaf[:, :3, :, None]
    dist_sq = lax.optimization_barrier(jnp.sum(offset * offset, axis=1))
    softened = dist_sq + SOFTENING
    taper = jnp.maximum(1.0 - dist_sq / CUTOFF_SQ, 0.0)
    kernel = taper * taper / (softened * jnp.sqrt(softened))
    on_left = lax.optimization_barrier(jnp.sum(offset * (kernel * right_leaf[:, 3, None, :])[:, None], axis=3))
    on_right = -lax.optimization_barrier(jnp.sum(offset * (kernel * left_leaf[:, 3, :, None])[:, None], axis=2))
    return (on_left, on_right)

def blocked_forces(left_leaf, right_leaf):
    count = left_leaf.shape[0]
    block_size = 32 if count % 32 == 0 else count
    shaped_left = left_leaf.reshape((count // block_size, block_size) + left_leaf.shape[1:])
    shaped_right = right_leaf.reshape((count // block_size, block_size) + right_leaf.shape[1:])
    force_left, force_right = lax.map(lambda pair: pair_forces(pair[0], pair[1]), (shaped_left, shaped_right))
    return (force_left.reshape((count, 3, LEAF)), force_right.reshape((count, 3, LEAF)))

def reference(positions, velocities, masses, time_bins, pair_owner, pair_slot, local_pairs):
    current = positions
    moving = velocities
    accel = jnp.zeros_like(positions)
    for subcycle in range(2):
        leaves = jnp.concatenate([current.reshape(3, NLEAF, LEAF), masses.reshape(1, NLEAF, LEAF)], axis=0).transpose(1, 0, 2)
        remote = pair_owner[subcycle] * L_DEV + pair_slot[subcycle]
        base_rows = (jnp.arange(LOCALS, dtype=jnp.int32) // LOCAL_DEV * L_DEV).astype(jnp.int32)
        local_ids = local_pairs[subcycle] + base_rows[:, None]
        all_pairs = jnp.concatenate([remote.reshape(DEVICES, PAIRS_DEV, 2), local_ids.reshape(DEVICES, LOCAL_DEV, 2)], axis=1)

        def add_device(total, leaf_ids):
            force_left, force_right = blocked_forces(leaves[leaf_ids[:, 0]], leaves[leaf_ids[:, 1]])
            total = total.at[leaf_ids[:, 0]].add(force_left)
            total = total.at[leaf_ids[:, 1]].add(force_right)
            return (total, None)
        summed, _ = lax.scan(add_device, jnp.zeros((NLEAF, 3, LEAF), jnp.float32), all_pairs)
        accel = summed.transpose(1, 0, 2).reshape(3, NPART)
        active = (time_bins >= 3 - subcycle).astype(jnp.float32)
        moving = moving + TIME_STEP * accel * active[None, :]
        current = current + TIME_STEP * moving
    return (current, moving, accel)
```

```python
import jax
import jax.numpy as jnp
from jax import lax
from jax.experimental import pallas as pl
from jax.experimental.pallas import tpu as pltpu
from jax.sharding import PartitionSpec as P

LEAF = 128
NLEAF = 64
DEVICES = 128
CAP = 4
PAIRS = 128
LOCAL = 64
SLOTS = DEVICES * CAP
AXES = ("gx", "gy", "gz")

SOFTENING = 0.01
CUTOFF_SQ = 0.04
TIME_STEP = 0.05
CENTRE = 0.5

F32 = jnp.float32
BF16 = jnp.bfloat16
NT = (((1,), (1,)), ((), ()))
NN = (((1,), (0,)), ((), ()))
TN = (((0,), (0,)), ((), ()))
VMEM = pl.BlockSpec(memory_space=pltpu.VMEM)


def split3(value):
    high = value.astype(BF16).astype(F32)
    rest = value - high
    middle = rest.astype(BF16).astype(F32)
    return high, middle, rest - middle


def leaf_parts(tile, row):
    xyz = jnp.where(row < 3, tile - CENTRE, 0.0)
    high, middle, low = split3(xyz)
    norm = split3(jnp.sum(xyz * xyz, axis=0, keepdims=True))
    mass = tile[3:4] * (1.0 / CUTOFF_SQ**2)
    moment = jnp.where(row < 3, xyz * mass, jnp.where(row == 3, mass, 0.0))
    mh, mm, ml = split3(moment)
    weights = jnp.concatenate([mh + pltpu.roll(mm, 4, 0), ml], axis=0).astype(BF16)
    return xyz, (high, middle, low), norm, weights


def squared_distances(left, right, row):
    _, (ah, am, al), (an0, an1, an2), _ = left
    _, (bh, bm, bl), (bn0, bn1, bn2), _ = right
    a_norm = jnp.where(
        row == 0, an0, jnp.where(row == 1, an1, jnp.where(row == 2, an2, jnp.where(row < 6, 1.0, 0.0)))
    )
    b_norm = jnp.where(
        row < 3, 1.0, jnp.where(row == 3, bn0, jnp.where(row == 4, bn1, jnp.where(row == 5, bn2, 0.0)))
    )
    bh, bm, bl = -2.0 * bh, -2.0 * bm, -2.0 * bl
    zero = jnp.zeros_like(a_norm)
    lhs = jnp.concatenate([ah, ah, am, ah, al, am, a_norm, zero], axis=0).astype(BF16)
    rhs = jnp.concatenate([bh, bm, bh, bl, bh, bm, b_norm, zero], axis=0).astype(BF16)
    return lax.dot_general(lhs, rhs, TN, preferred_element_type=F32)


def pair_kernel(dist_sq):
    taper = jnp.maximum(CUTOFF_SQ - dist_sq, 0.0)
    root = lax.rsqrt(dist_sq + SOFTENING)
    scaled = taper * root
    kernel = scaled * scaled * root
    high = kernel.astype(BF16)
    return high, (kernel - high.astype(F32)).astype(BF16)


def moments(left, right, kernel):
    high, low = kernel
    rows = jnp.concatenate([high, low], axis=0)
    columns = jnp.concatenate([high, low], axis=1)
    on_left = lax.dot_general(right[3], rows, NT, preferred_element_type=F32)
    on_right = lax.dot_general(left[3], columns, NN, preferred_element_type=F32)
    return (on_left[:, :LEAF] + on_left[:, LEAF:], on_right[:, :LEAF] + on_right[:, LEAF:])


def force_tile(moment, xyz):
    total = moment[0:8] + moment[8:16]
    total = total + pltpu.roll(total, 4, 0)
    return total - (xyz + pltpu.roll(xyz, 4, 0)) * total[3:4]


def pair_forces(tiles, row):
    parts = [(leaf_parts(a, row), leaf_parts(b, row)) for a, b in tiles]
    dists = [squared_distances(a, b, row) for a, b in parts]
    kernels = [pair_kernel(q) for q in dists]
    sums = [moments(a, b, k) for (a, b), k in zip(parts, kernels)]
    return [
        (force_tile(fa, a[0]), force_tile(fb, b[0])) for (a, b), (fa, fb) in zip(parts, sums)
    ]


def row_iota():
    return lax.broadcasted_iota(jnp.int32, (8, LEAF), 0)


def fill_slots(asked, state, looked):
    row = row_iota()

    def body(step, carry):
        for u in range(16):
            tile = step * 16 + u
            looked[pl.ds(pl.multiple_of(tile * 8, 8), 8), :] = jnp.where(
                row < 4, state[asked[2 * tile]], state[asked[2 * tile + 1]]
            )
        return carry

    lax.fori_loop(0, SLOTS // 32, body, 0)


def pack_kernel(positions, velocities, masses, state, moving):
    for leaf in range(NLEAF):
        lanes = slice(leaf * LEAF, (leaf + 1) * LEAF)
        state[leaf, 0:3, :] = positions[:, lanes]
        state[leaf, 4:7, :] = positions[:, lanes]
        state[leaf, 3:4, :] = masses[leaf : leaf + 1, :]
        state[leaf, 7:8, :] = masses[leaf : leaf + 1, :]
        moving[leaf, 0:3, :] = velocities[:, lanes]
        moving[leaf, 4:7, :] = velocities[:, lanes]
        moving[leaf, 3:4, :] = jnp.zeros((1, LEAF), F32)
        moving[leaf, 7:8, :] = jnp.zeros((1, LEAF), F32)
    state[NLEAF] = jnp.zeros((8, LEAF), F32)


def gather_kernel(asked, state, looked):
    fill_slots(asked, state, looked)


def local_kernel(pairs, state, forces):
    row = row_iota()
    forces[...] = jnp.zeros_like(forces)
    unroll = 16

    def body(step, carry):
        ids = [
            (pairs[2 * (step * unroll + u)], pairs[2 * (step * unroll + u) + 1])
            for u in range(unroll)
        ]
        found = pair_forces([(state[a], state[b]) for a, b in ids], row)
        for (a, b), (fa, fb) in zip(ids, found):
            forces[a] += fa
            forces[b] += fb
        return carry

    lax.fori_loop(0, LOCAL // unroll, body, 0)


def remote_kernel(placed, arrived, pushed):
    row = row_iota()
    pushed[...] = jnp.zeros_like(pushed)
    unroll = 16

    def leaf(slot):
        tile = arrived[pl.ds(pl.multiple_of((slot >> 1) * 8, 8), 8), :]
        return jnp.where((slot & 1) == 1, pltpu.roll(tile, 4, 0), tile)

    def body(step, carry):
        ids = [
            (placed[2 * (step * unroll + u)], placed[2 * (step * unroll + u) + 1])
            for u in range(unroll)
        ]
        found = pair_forces([(leaf(a), leaf(b)) for a, b in ids], row)
        for (a, b), (fa, fb) in zip(ids, found):
            pushed[pl.ds(3 * a, 3), :] = fa[0:3]
            pushed[pl.ds(3 * b, 3), :] = fb[0:3]
        return carry

    lax.fori_loop(0, PAIRS // unroll, body, 0)


def summed_tiles(codes, returned):
    target = lax.broadcasted_iota(jnp.int32, (4 * NLEAF, 3 * SLOTS), 0)
    chosen = jnp.where(target == codes[...], 1.0, 0.0).astype(BF16)
    total = jnp.zeros((4 * NLEAF, LEAF), F32)
    for part in split3(returned[...]):
        total = total + lax.dot_general(chosen, part.astype(BF16), NN, preferred_element_type=F32)
    return total


def kick_drift(threshold, codes, returned, local, state, moving, bins, leaf_done):
    row = row_iota()
    total = summed_tiles(codes, returned)
    for leaf in range(NLEAF):
        pair = total[leaf // 2 * 8 : leaf // 2 * 8 + 8]
        other = pltpu.roll(pair, 4, 0)
        mine = jnp.where(row < 4, pair, other) if leaf % 2 == 0 else jnp.where(row < 4, other, pair)
        accel = jnp.where((row & 3) < 3, mine + local[leaf], 0.0)
        active = bins[leaf : leaf + 1, :] >= threshold
        velocity = moving[leaf] + jnp.where(active, TIME_STEP * accel, 0.0)
        position = state[leaf] + TIME_STEP * velocity
        leaf_done(leaf, position, velocity, accel)


def advance_kernel(asked, codes, returned, local, state, moving, bins, looked, new_state, new_moving):
    def leaf_done(leaf, position, velocity, accel):
        new_state[leaf] = position
        new_moving[leaf] = velocity

    kick_drift(3, codes, returned, local, state, moving, bins, leaf_done)
    new_state[NLEAF] = jnp.zeros((8, LEAF), F32)
    fill_slots(asked, new_state, looked)


def finish_kernel(codes, returned, local, state, moving, bins, positions, velocities, accels):
    def leaf_done(leaf, position, velocity, accel):
        lanes = slice(leaf * LEAF, (leaf + 1) * LEAF)
        positions[:, lanes] = position[0:3]
        velocities[:, lanes] = velocity[0:3]
        accels[:, lanes] = accel[0:3]

    kick_drift(2, codes, returned, local, state, moving, bins, leaf_done)


def call(kernel, out_shapes, scalars, arrays, flops, size):
    return pl.pallas_call(
        kernel,
        out_shape=out_shapes,
        grid_spec=pltpu.PrefetchScalarGridSpec(
            num_scalar_prefetch=len(scalars),
            grid=(),
            in_specs=[VMEM] * len(arrays),
            out_specs=jax.tree.map(lambda _: VMEM, out_shapes),
        ),
        compiler_params=pltpu.CompilerParams(vmem_limit_bytes=40 * 2**20),
        cost_estimate=pl.CostEstimate(flops=flops, bytes_accessed=size, transcendentals=0),
    )(*scalars, *arrays)


def shape(*dims):
    return jax.ShapeDtypeStruct(dims, F32)


def exchange(array):
    return lax.all_to_all(array, AXES, split_axis=0, concat_axis=0, tiled=True)


def send_leaves(looked):
    return exchange(looked.reshape(DEVICES, 4 * CAP, LEAF)).reshape(4 * SLOTS, LEAF)


def send_forces(pushed):
    return exchange(pushed.reshape(DEVICES, 3, CAP, LEAF)).reshape(3 * SLOTS, LEAF)


def requests(pair_owner, pair_slot):
    owners = pair_owner.reshape(2, 2 * PAIRS)
    slots = pair_slot.reshape(2, 2 * PAIRS)
    earlier = jnp.arange(2 * PAIRS)[None, :] < jnp.arange(2 * PAIRS)[:, None]
    rank = jnp.sum(
        ((owners[:, :, None] == owners[:, None, :]) & earlier[None]).astype(jnp.int32), axis=2
    )
    placed = owners * CAP + rank
    spots = jnp.arange(SLOTS, dtype=jnp.int32)
    wanted = NLEAF + jnp.sum(
        jnp.where(placed[:, :, None] == spots[None, None, :], (slots - NLEAF)[:, :, None], 0), axis=1
    )
    return placed, wanted.reshape(2, DEVICES, CAP).transpose(1, 0, 2).reshape(DEVICES, 2 * CAP)


def shards(positions, velocities, masses, time_bins, pair_owner, pair_slot, local_pairs):
    masses = masses.reshape(NLEAF, LEAF)
    bins = time_bins.reshape(NLEAF, LEAF)
    placed, wanted = requests(pair_owner, pair_slot)
    asked = exchange(wanted).reshape(DEVICES, 2, CAP).transpose(1, 0, 2).reshape(2, SLOTS)
    codes = (4 * asked[:, :, None] + jnp.arange(3, dtype=jnp.int32)).reshape(2, 1, 3 * SLOTS)
    local_ids = local_pairs.reshape(2, 2 * LOCAL)

    state_shape = shape(NLEAF + 1, 8, LEAF)
    moving_shape = shape(NLEAF, 8, LEAF)
    looked_shape = shape(4 * SLOTS, LEAF)
    pushed_shape = shape(3 * SLOTS, LEAF)

    def local_forces(ids, state):
        return call(local_kernel, moving_shape, [ids], [state], 64 * 2**14 * 25, 2**20)

    def remote_forces(ids, arrived):
        return call(remote_kernel, pushed_shape, [ids], [arrived], 128 * 2**14 * 25, 2**21)

    state, moving = call(
        pack_kernel, (state_shape, moving_shape), [], [positions, velocities, masses], 2**16, 2**20
    )
    local = local_forces(local_ids[0], state)
    looked = call(gather_kernel, looked_shape, [asked[0]], [state], 2**16, 2**21)
    pushed = remote_forces(placed[0], send_leaves(looked))
    returned = send_forces(pushed)
    looked, state, moving = call(
        advance_kernel,
        (looked_shape, state_shape, moving_shape),
        [asked[1]],
        [codes[0], returned, local, state, moving, bins],
        2**16,
        2**22,
    )
    local = local_forces(local_ids[1], state)
    pushed = remote_forces(placed[1], send_leaves(looked))
    returned = send_forces(pushed)
    out = shape(3, NLEAF * LEAF)
    return call(
        finish_kernel,
        (out, out, out),
        [],
        [codes[1], returned, local, state, moving, bins],
        2**16,
        2**22,
    )


def solution(mesh):
    split = P(None, AXES)
    rows = P(None, AXES, None)
    return jax.shard_map(
        shards,
        mesh=mesh,
        in_specs=(split, split, P(AXES), P(AXES), rows, rows, rows),
        out_specs=(split, split, split),
        check_vma=False,
    )
```

```python
import jax
import jax.numpy as jnp
from jax import lax
from jax.experimental import pallas as pl
from jax.experimental.pallas import tpu as pltpu
from jax.sharding import PartitionSpec as P

LEAF = 128
NLEAF = 64
DEVICES = 128
CAP = 4
PAIRS = 128
LOCAL = 64
SLOTS = DEVICES * CAP
AXES = ("gx", "gy", "gz")

SOFTENING = 0.01
CUTOFF_SQ = 0.04
TIME_STEP = 0.05
CENTRE = 0.5

F32 = jnp.float32
BF16 = jnp.bfloat16
NT = (((1,), (1,)), ((), ()))
NN = (((1,), (0,)), ((), ()))
TN = (((0,), (0,)), ((), ()))
VMEM = pl.BlockSpec(memory_space=pltpu.VMEM)


def split3(value):
    high = value.astype(BF16).astype(F32)
    rest = value - high
    middle = rest.astype(BF16).astype(F32)
    return high, middle, rest - middle


def pair_parts(tile, row):
    vector = (row & 3) < 3
    xyz = jnp.where(vector, tile - CENTRE, 0.0)
    parts = split3(xyz)
    square = xyz * xyz
    norm = pltpu.roll(square, 1, 0) + pltpu.roll(square, 2, 0) + pltpu.roll(square, 3, 0)
    norms = split3(norm + jnp.where(row == 3, SOFTENING, 0.0))
    mass = jnp.where(row < 4, tile[3:4], tile[7:8]) * (1.0 / CUTOFF_SQ**2)
    weights = split3(jnp.where(vector, xyz, 1.0) * mass)
    weights = jnp.concatenate([*weights, jnp.zeros_like(xyz)], axis=0).astype(BF16)
    return xyz, parts, norms, weights


def softened_distances(parts, norms, row):
    high, middle, low = parts
    minus_two = jnp.where(row < 3, -2.0, 0.0)
    h2, m2, l2 = (pltpu.roll(part, 4, 0) * minus_two for part in parts)
    lhs, rhs = [], []
    for left, right, norm in zip(parts, (h2, h2, h2), norms):
        lhs.append(left + jnp.where(row == 3, norm, jnp.where(row == 7, 1.0, 0.0)))
        rhs.append(right + jnp.where(row == 7, norm, jnp.where(row == 3, 1.0, 0.0)))
    lhs = jnp.concatenate(lhs + [high, high, middle], axis=0).astype(BF16)
    rhs = jnp.concatenate(rhs + [m2, l2, m2], axis=0).astype(BF16)
    return lax.dot_general(lhs, rhs, TN, preferred_element_type=F32)


def pair_kernel(softened):
    taper = jnp.maximum((CUTOFF_SQ + SOFTENING) - softened, 0.0)
    root = lax.rsqrt(softened)
    scaled = taper * root
    kernel = scaled * scaled * root
    high = kernel.astype(BF16)
    return high, (kernel - high.astype(F32)).astype(BF16)


def moments(weights, kernel):
    high, low = kernel
    twice = jnp.concatenate([weights, weights], axis=1)
    on_left = lax.dot_general(
        jnp.concatenate([high, low], axis=1), twice, NT, preferred_element_type=F32
    ).T
    on_right = lax.dot_general(
        twice, jnp.concatenate([high, low], axis=0), NN, preferred_element_type=F32
    )
    return on_left, on_right


def force_tile(sums, xyz, row):
    on_left, on_right = (part[0:8] + part[8:16] + part[16:24] for part in sums)
    total = jnp.where(row < 4, on_right, on_left)
    mass = jnp.where(row < 4, total[3:4], total[7:8])
    return total - pltpu.roll(xyz, 4, 0) * mass


def pair_forces(tiles, row):
    count, lag = len(tiles), 4
    parts, dists, sums, out = {}, {}, {}, []
    for step in range(count + 2 * lag):
        if step < count:
            parts[step] = pair_parts(tiles[step], row)
            dists[step] = softened_distances(parts[step][1], parts[step][2], row)
        k = step - lag
        if 0 <= k < count:
            sums[k] = moments(parts[k][3], pair_kernel(dists[k]))
        k = step - 2 * lag
        if k >= 0:
            out.append(force_tile(sums[k], parts[k][0], row))
    return out


def row_iota():
    return lax.broadcasted_iota(jnp.int32, (8, LEAF), 0)


def fill_slots(asked, state, looked):
    row = row_iota()

    def body(step, carry):
        for u in range(16):
            tile = step * 16 + u
            looked[pl.ds(pl.multiple_of(tile * 8, 8), 8), :] = jnp.where(
                row < 4, state[asked[2 * tile]], state[asked[2 * tile + 1]]
            )
        return carry

    lax.fori_loop(0, SLOTS // 32, body, 0)


def pack_kernel(positions, velocities, masses, state, moving):
    for leaf in range(NLEAF):
        lanes = slice(leaf * LEAF, (leaf + 1) * LEAF)
        state[leaf, 0:3, :] = positions[:, lanes]
        state[leaf, 4:7, :] = positions[:, lanes]
        state[leaf, 3:4, :] = masses[leaf : leaf + 1, :]
        state[leaf, 7:8, :] = masses[leaf : leaf + 1, :]
        moving[leaf, 0:3, :] = velocities[:, lanes]
        moving[leaf, 4:7, :] = velocities[:, lanes]
        moving[leaf, 3:4, :] = jnp.zeros((1, LEAF), F32)
        moving[leaf, 7:8, :] = jnp.zeros((1, LEAF), F32)
    state[NLEAF] = jnp.zeros((8, LEAF), F32)


def gather_kernel(asked, state, looked):
    fill_slots(asked, state, looked)


def local_kernel(pairs, state, forces):
    row = row_iota()
    forces[...] = jnp.zeros_like(forces)
    unroll = 32

    def body(step, carry):
        ids = [
            (pairs[0, step * unroll + u], pairs[1, step * unroll + u])
            for u in range(unroll)
        ]
        found = pair_forces([jnp.where(row < 4, state[a], state[b]) for a, b in ids], row)
        for (a, b), force in zip(ids, found):
            forces[a] += jnp.where(row < 4, 0.0, force)
            forces[b] += jnp.where(row < 4, force, 0.0)
        return carry

    lax.fori_loop(0, LOCAL // unroll, body, 0)
    for leaf in range(NLEAF):
        forces[leaf] += pltpu.roll(forces[leaf], 4, 0)


def remote_kernel(placed, arrived, pushed):
    row = row_iota()
    pushed[...] = jnp.zeros_like(pushed)
    unroll = 64

    def leaf(slot, half):
        tile = arrived[pl.ds(pl.multiple_of((slot >> 1) * 8, 8), 8), :]
        return jnp.where((slot & 1) == half, tile, pltpu.roll(tile, 4, 0))

    def body(step, carry):
        ids = [
            (placed[0, step * unroll + u], placed[1, step * unroll + u])
            for u in range(unroll)
        ]
        found = pair_forces([jnp.where(row < 4, leaf(a, 0), leaf(b, 1)) for a, b in ids], row)
        for (a, b), force in zip(ids, found):
            pushed[pl.ds(3 * a, 3), :] = force[4:7]
            pushed[pl.ds(3 * b, 3), :] = force[0:3]
        return carry

    lax.fori_loop(0, PAIRS // unroll, body, 0)


def summed_tiles(codes, returned):
    target = lax.broadcasted_iota(jnp.int32, (4 * NLEAF, 3 * SLOTS), 0)
    chosen = jnp.where(target == codes[...], 1.0, 0.0).astype(BF16)
    total = jnp.zeros((4 * NLEAF, LEAF), F32)
    for part in split3(returned[...]):
        total = total + lax.dot_general(chosen, part.astype(BF16), NN, preferred_element_type=F32)
    return total


def kick_drift(threshold, codes, returned, local, state, moving, bins, leaf_done):
    row = row_iota()
    total = summed_tiles(codes, returned)
    for leaf in range(NLEAF):
        pair = total[leaf // 2 * 8 : leaf // 2 * 8 + 8]
        other = pltpu.roll(pair, 4, 0)
        mine = jnp.where(row < 4, pair, other) if leaf % 2 == 0 else jnp.where(row < 4, other, pair)
        accel = jnp.where((row & 3) < 3, mine + local[leaf], 0.0)
        active = bins[leaf : leaf + 1, :] >= threshold
        velocity = moving[leaf] + jnp.where(active, TIME_STEP * accel, 0.0)
        position = state[leaf] + TIME_STEP * velocity
        leaf_done(leaf, position, velocity, accel)


def advance_kernel(asked, codes, returned, local, state, moving, bins, looked, new_state, new_moving):
    def leaf_done(leaf, position, velocity, accel):
        new_state[leaf] = position
        new_moving[leaf] = velocity

    kick_drift(3, codes, returned, local, state, moving, bins, leaf_done)
    new_state[NLEAF] = jnp.zeros((8, LEAF), F32)
    fill_slots(asked, new_state, looked)


def finish_kernel(codes, returned, local, state, moving, bins, positions, velocities, accels):
    def leaf_done(leaf, position, velocity, accel):
        lanes = slice(leaf * LEAF, (leaf + 1) * LEAF)
        positions[:, lanes] = position[0:3]
        velocities[:, lanes] = velocity[0:3]
        accels[:, lanes] = accel[0:3]

    kick_drift(2, codes, returned, local, state, moving, bins, leaf_done)


def call(kernel, out_shapes, scalars, arrays, flops, size):
    return pl.pallas_call(
        kernel,
        out_shape=out_shapes,
        grid_spec=pltpu.PrefetchScalarGridSpec(
            num_scalar_prefetch=len(scalars),
            grid=(),
            in_specs=[VMEM] * len(arrays),
            out_specs=jax.tree.map(lambda _: VMEM, out_shapes),
        ),
        compiler_params=pltpu.CompilerParams(vmem_limit_bytes=40 * 2**20),
        cost_estimate=pl.CostEstimate(flops=flops, bytes_accessed=size, transcendentals=0),
    )(*scalars, *arrays)


def shape(*dims):
    return jax.ShapeDtypeStruct(dims, F32)


def exchange(array):
    return lax.all_to_all(array, AXES, split_axis=0, concat_axis=0, tiled=True)


def send_leaves(looked):
    return exchange(looked.reshape(DEVICES, 4 * CAP, LEAF)).reshape(4 * SLOTS, LEAF)


def send_forces(pushed):
    return exchange(pushed.reshape(DEVICES, 3, CAP, LEAF)).reshape(3 * SLOTS, LEAF)


def request_kernel(owners, slots, placed0, placed1, wanted):
    ends = 2 * PAIRS
    owner_of = lax.broadcasted_iota(jnp.int32, (DEVICES, ends), 0)
    earlier = lax.broadcasted_iota(jnp.int32, (ends, ends), 0) < lax.broadcasted_iota(
        jnp.int32, (ends, ends), 1
    )
    earlier = jnp.where(earlier, 1.0, 0.0).astype(BF16)
    column = lax.broadcasted_iota(jnp.int32, (ends, LEAF), 1)
    total = jnp.zeros((DEVICES, LEAF), F32)
    for sub, placed in enumerate((placed0, placed1)):
        owner = jnp.concatenate([owners[sub, 0:1], owners[sub, 1:2]], axis=1)
        slot = jnp.concatenate([slots[sub, 0:1], slots[sub, 1:2]], axis=1) - NLEAF
        hit = jnp.where(owner_of == owner, 1.0, 0.0)
        before = lax.dot_general(hit.astype(BF16), earlier, NN, preferred_element_type=F32)
        rank = jnp.sum(hit * before, axis=0, keepdims=True)
        place = CAP * owner + rank.astype(jnp.int32)
        placed[0:1, :] = place[:, :PAIRS]
        placed[1:2, :] = place[:, PAIRS:]
        asked = hit * slot.astype(F32)
        for turn in range(CAP):
            mine = jnp.where(before == float(turn), asked, 0.0).astype(BF16)
            here = jnp.where(column == CAP * sub + turn, 1.0, 0.0).astype(BF16)
            total += lax.dot_general(mine, here, NN, preferred_element_type=F32)
    wanted[...] = total.astype(jnp.int32) + NLEAF


def shards(positions, velocities, masses, time_bins, pair_owner, pair_slot, local_pairs):
    masses = masses.reshape(NLEAF, LEAF)
    bins = time_bins.reshape(NLEAF, LEAF)
    ints = jax.ShapeDtypeStruct((2, PAIRS), jnp.int32)
    *placed, wanted = call(
        request_kernel,
        (ints, ints, jax.ShapeDtypeStruct((DEVICES, LEAF), jnp.int32)),
        [],
        [pair_owner.transpose(0, 2, 1), pair_slot.transpose(0, 2, 1)],
        2**26,
        2**18,
    )
    asked = exchange(wanted.reshape(DEVICES, 1, LEAF)).reshape(DEVICES, LEAF)[:, : 2 * CAP]
    asked = asked.reshape(DEVICES, 2, CAP).transpose(1, 0, 2).reshape(2, SLOTS)
    codes = (4 * asked[:, :, None] + jnp.arange(3, dtype=jnp.int32)).reshape(2, 1, 3 * SLOTS)
    local_ids = local_pairs.transpose(0, 2, 1)

    state_shape = shape(NLEAF + 1, 8, LEAF)
    moving_shape = shape(NLEAF, 8, LEAF)
    looked_shape = shape(4 * SLOTS, LEAF)
    pushed_shape = shape(3 * SLOTS, LEAF)

    def local_forces(ids, state):
        return call(local_kernel, moving_shape, [ids], [state], 64 * 2**14 * 25, 2**20)

    def remote_forces(ids, arrived):
        return call(remote_kernel, pushed_shape, [ids], [arrived], 128 * 2**14 * 25, 2**21)

    state, moving = call(
        pack_kernel, (state_shape, moving_shape), [], [positions, velocities, masses], 2**16, 2**20
    )
    local = local_forces(local_ids[0], state)
    looked = call(gather_kernel, looked_shape, [asked[0]], [state], 2**16, 2**21)
    pushed = remote_forces(placed[0], send_leaves(looked))
    returned = send_forces(pushed)
    looked, state, moving = call(
        advance_kernel,
        (looked_shape, state_shape, moving_shape),
        [asked[1]],
        [codes[0], returned, local, state, moving, bins],
        2**16,
        2**22,
    )
    local = local_forces(local_ids[1], state)
    pushed = remote_forces(placed[1], send_leaves(looked))
    returned = send_forces(pushed)
    out = shape(3, NLEAF * LEAF)
    return call(
        finish_kernel,
        (out, out, out),
        [],
        [codes[1], returned, local, state, moving, bins],
        2**16,
        2**22,
    )


def solution(mesh):
    split = P(None, AXES)
    rows = P(None, AXES, None)
    return jax.shard_map(
        shards,
        mesh=mesh,
        in_specs=(split, split, P(AXES), P(AXES), rows, rows, rows),
        out_specs=(split, split, split),
        check_vma=False,
    )
```

```python
import jax
import jax.numpy as jnp
from jax import lax
from jax.experimental import pallas as pl
from jax.experimental.pallas import tpu as pltpu
from jax.sharding import PartitionSpec as P

LEAF = 128
NLEAF = 64
DEVICES = 128
CAP = 4
PAIRS = 128
LOCAL = 64
SLOTS = DEVICES * CAP
AXES = ("gx", "gy", "gz")

SOFTENING = 0.01
CUTOFF_SQ = 0.04
TIME_STEP = 0.05
CENTRE = 0.5

F32 = jnp.float32
BF16 = jnp.bfloat16
NT = (((1,), (1,)), ((), ()))
NN = (((1,), (0,)), ((), ()))
TN = (((0,), (0,)), ((), ()))
VMEM = pl.BlockSpec(memory_space=pltpu.VMEM)


def split3(value):
    high = value.astype(BF16).astype(F32)
    rest = value - high
    middle = rest.astype(BF16).astype(F32)
    return high, middle, rest - middle


def pair_parts(tile, row):
    vector = (row & 3) < 3
    xyz = jnp.where(vector, tile - CENTRE, 0.0)
    parts = split3(xyz)
    square = xyz * xyz
    norm = pltpu.roll(square, 1, 0) + pltpu.roll(square, 2, 0) + pltpu.roll(square, 3, 0)
    norms = split3(norm + jnp.where(row == 3, SOFTENING, 0.0))
    mass = jnp.where(row < 4, tile[3:4], tile[7:8]) * (1.0 / CUTOFF_SQ**2)
    weights = split3(jnp.where(vector, xyz, 1.0) * mass)
    weights = jnp.concatenate([*weights, jnp.zeros_like(xyz)], axis=0).astype(BF16)
    return xyz, parts, norms, weights


def softened_distances(parts, norms, row):
    high, middle, low = parts
    minus_two = jnp.where(row < 3, -2.0, 0.0)
    h2, m2, l2 = (pltpu.roll(part, 4, 0) * minus_two for part in parts)
    lhs, rhs = [], []
    for left, right, norm in zip(parts, (h2, h2, h2), norms):
        lhs.append(left + jnp.where(row == 3, norm, jnp.where(row == 7, 1.0, 0.0)))
        rhs.append(right + jnp.where(row == 7, norm, jnp.where(row == 3, 1.0, 0.0)))
    lhs = jnp.concatenate(lhs + [high, high, middle], axis=0).astype(BF16)
    rhs = jnp.concatenate(rhs + [m2, l2, m2], axis=0).astype(BF16)
    return lax.dot_general(lhs, rhs, TN, preferred_element_type=F32)


def pair_kernel(softened):
    taper = jnp.maximum((CUTOFF_SQ + SOFTENING) - softened, 0.0)
    root = lax.rsqrt(softened)
    scaled = taper * root
    kernel = scaled * scaled * root
    high = kernel.astype(BF16)
    return high, (kernel - high.astype(F32)).astype(BF16)


def moments(weights, kernel):
    high, low = kernel
    twice = jnp.concatenate([weights, weights], axis=1)
    on_left = lax.dot_general(
        jnp.concatenate([high, low], axis=1), twice, NT, preferred_element_type=F32
    ).T
    on_right = lax.dot_general(
        twice, jnp.concatenate([high, low], axis=0), NN, preferred_element_type=F32
    )
    return on_left, on_right


def force_tile(sums, xyz, row):
    on_left, on_right = (part[0:8] + part[8:16] + part[16:24] for part in sums)
    total = jnp.where(row < 4, on_right, on_left)
    mass = jnp.where(row < 4, total[3:4], total[7:8])
    return total - pltpu.roll(xyz, 4, 0) * mass


def pair_forces(tiles, row):
    count, lag = len(tiles), 4
    parts, dists, sums, out = {}, {}, {}, []
    for step in range(count + 2 * lag):
        if step < count:
            parts[step] = pair_parts(tiles[step], row)
            dists[step] = softened_distances(parts[step][1], parts[step][2], row)
        k = step - lag
        if 0 <= k < count:
            sums[k] = moments(parts[k][3], pair_kernel(dists[k]))
        k = step - 2 * lag
        if k >= 0:
            out.append(force_tile(sums[k], parts[k][0], row))
    return out


def row_iota():
    return lax.broadcasted_iota(jnp.int32, (8, LEAF), 0)


def leaf_tile(state, leaf):
    return state[pl.ds(pl.multiple_of(leaf * 8, 8), 8), :]


def fill_slots(first, asked, state, looked):
    row = row_iota()

    def body(step, carry):
        for u in range(8):
            worker = step * 8 + u
            for half in range(2):
                left = leaf_tile(state, asked[first + 2 * half, worker])
                right = leaf_tile(state, asked[first + 2 * half + 1, worker])
                looked[pl.ds(pl.multiple_of(worker * 16 + half * 8, 8), 8), :] = jnp.where(
                    row < 4, left, right
                )
        return carry

    lax.fori_loop(0, DEVICES // 8, body, 0)


def component(index):
    return slice(index * NLEAF, (index + 1) * NLEAF)


def store_state(state, index, value):
    state[pl.ds(index, NLEAF, stride=8), :] = value
    state[pl.ds(index + 4, NLEAF, stride=8), :] = value


def pack_kernel(positions, velocities, masses, state, where, moving):
    for leaf in range(NLEAF):
        lanes = slice(leaf * LEAF, (leaf + 1) * LEAF)
        where[pl.ds(leaf, 3, stride=NLEAF), :] = positions[:, lanes]
        moving[pl.ds(leaf, 3, stride=NLEAF), :] = velocities[:, lanes]
    for index in range(3):
        store_state(state, index, where[component(index), :])
    store_state(state, 3, masses[...])
    state[8 * NLEAF :, :] = jnp.zeros((8, LEAF), F32)


def gather_kernel(wanted, state, _, looked, asked, scalars, sem):
    asked[...] = wanted[...].T[: 2 * CAP]
    copy = pltpu.make_async_copy(asked, scalars, sem)
    copy.start()
    copy.wait()
    fill_slots(0, scalars, state, looked)


def local_kernel(pairs, state, forces):
    row = row_iota()
    forces[...] = jnp.zeros_like(forces)
    unroll = 32

    def body(step, carry):
        ids = [
            (pairs[0, step * unroll + u], pairs[1, step * unroll + u])
            for u in range(unroll)
        ]
        found = pair_forces([jnp.where(row < 4, leaf_tile(state, a), leaf_tile(state, b)) for a, b in ids], row)
        for (a, b), force in zip(ids, found):
            to_left = pl.ds(pl.multiple_of(a * 8, 8), 8)
            to_right = pl.ds(pl.multiple_of(b * 8, 8), 8)
            forces[to_left, :] += jnp.where(row < 4, 0.0, force)
            forces[to_right, :] += jnp.where(row < 4, force, 0.0)
        return carry

    lax.fori_loop(0, LOCAL // unroll, body, 0)


def remote_kernel(places, arrived, pushed, placed, sem):
    row = row_iota()
    copy = pltpu.make_async_copy(places, placed, sem)
    copy.start()
    pushed[...] = jnp.zeros_like(pushed)
    copy.wait()
    unroll = 64

    def leaf(slot, half):
        tile = arrived[pl.ds(pl.multiple_of((slot >> 1) * 8, 8), 8), :]
        return jnp.where((slot & 1) == half, tile, pltpu.roll(tile, 4, 0))

    def body(step, carry):
        ids = [
            (placed[0, step * unroll + u], placed[1, step * unroll + u])
            for u in range(unroll)
        ]
        found = pair_forces([jnp.where(row < 4, leaf(a, 0), leaf(b, 1)) for a, b in ids], row)
        for (a, b), force in zip(ids, found):
            pushed[pl.ds(3 * a, 3), :] = force[4:7]
            pushed[pl.ds(3 * b, 3), :] = force[0:3]
        return carry

    lax.fori_loop(0, PAIRS // unroll, body, 0)


def summed(first, asked, returned):
    target = lax.broadcasted_iota(jnp.int32, (NLEAF, DEVICES), 0)
    chosen, blocks = [], []
    for turn in range(CAP):
        chosen.append(jnp.where(target == asked[first + turn : first + turn + 1, :], 1.0, 0.0))
        rows = [
            returned[pl.ds(3 * turn + index, DEVICES, stride=3 * CAP), :] for index in range(3)
        ]
        blocks.append(jnp.concatenate(rows, axis=1))
    chosen = jnp.concatenate(chosen, axis=1).astype(BF16)
    total = jnp.zeros((NLEAF, 3 * LEAF), F32)
    for part in split3(jnp.concatenate(blocks, axis=0)):
        total += lax.dot_general(chosen, part.astype(BF16), NN, preferred_element_type=F32)
    return total


def kick_drift(subcycle, asked, returned, local, where, moving, bins):
    total = summed(CAP * subcycle, asked, returned)
    active = bins[...] >= 3 - subcycle
    for index in range(3):
        accel = total[:, index * LEAF : (index + 1) * LEAF]
        accel += local[pl.ds(index, NLEAF, stride=8), :] + local[pl.ds(index + 4, NLEAF, stride=8), :]
        velocity = moving[component(index), :] + jnp.where(active, TIME_STEP * accel, 0.0)
        yield index, accel, velocity, where[component(index), :] + TIME_STEP * velocity


def advance_kernel(
    asked, returned, local, masses, where, moving, bins, looked, state, new_where, new_moving, scalars, sem
):
    copy = pltpu.make_async_copy(asked, scalars, sem)
    copy.start()
    store_state(state, 3, masses[...])
    state[8 * NLEAF :, :] = jnp.zeros((8, LEAF), F32)
    for index, _, velocity, position in kick_drift(0, asked, returned, local, where, moving, bins):
        new_moving[component(index), :] = velocity
        new_where[component(index), :] = position
        store_state(state, index, position)
    copy.wait()
    fill_slots(CAP, scalars, state, looked)


def finish_kernel(asked, returned, local, where, moving, bins, positions, velocities, accels, rows):
    for index, *results in kick_drift(1, asked, returned, local, where, moving, bins):
        for number, result in enumerate(results):
            rows[number, component(index), :] = result
    for leaf in range(NLEAF):
        lanes = slice(leaf * LEAF, (leaf + 1) * LEAF)
        for number, out in enumerate((accels, velocities, positions)):
            out[:, lanes] = rows[number, pl.ds(leaf, 3, stride=NLEAF), :]


def call(kernel, out_shapes, arrays, flops, size, scratch=(), in_specs=None, scalars=()):
    return pl.pallas_call(
        kernel,
        out_shape=out_shapes,
        grid_spec=pltpu.PrefetchScalarGridSpec(
            num_scalar_prefetch=len(scalars),
            grid=(),
            in_specs=in_specs or [VMEM] * len(arrays),
            out_specs=jax.tree.map(lambda _: VMEM, out_shapes),
            scratch_shapes=scratch,
        ),
        compiler_params=pltpu.CompilerParams(vmem_limit_bytes=40 * 2**20),
        cost_estimate=pl.CostEstimate(flops=flops, bytes_accessed=size, transcendentals=0),
    )(*scalars, *arrays)


def shape(*dims, dtype=F32):
    return jax.ShapeDtypeStruct(dims, dtype)


def exchange(array):
    return lax.all_to_all(array, AXES, split_axis=0, concat_axis=0, tiled=True)


def send_leaves(looked):
    return exchange(looked.reshape(DEVICES, 4 * CAP, LEAF)).reshape(4 * SLOTS, LEAF)


def send_forces(pushed):
    return exchange(pushed.reshape(DEVICES, 3, CAP, LEAF)).reshape(3 * SLOTS, LEAF)


def request_kernel(pair_owner, pair_slot, placed0, placed1, wanted, owners, slots, sems):
    copies = [
        pltpu.make_async_copy(pair_owner, owners, sems.at[0]),
        pltpu.make_async_copy(pair_slot, slots, sems.at[1]),
    ]
    for copy in copies:
        copy.start()
    for copy in copies:
        copy.wait()
    ends = 2 * PAIRS
    owner_of = lax.broadcasted_iota(jnp.int32, (DEVICES, ends), 0)
    earlier = lax.broadcasted_iota(jnp.int32, (ends, ends), 0) < lax.broadcasted_iota(
        jnp.int32, (ends, ends), 1
    )
    earlier = jnp.where(earlier, 1.0, 0.0).astype(BF16)
    column = lax.broadcasted_iota(jnp.int32, (ends, LEAF), 1)
    total = jnp.zeros((DEVICES, LEAF), F32)
    for sub, placed in enumerate((placed0, placed1)):
        owner = jnp.concatenate([owners[sub, 0:1], owners[sub, 1:2]], axis=1)
        slot = jnp.concatenate([slots[sub, 0:1], slots[sub, 1:2]], axis=1) - NLEAF
        hit = jnp.where(owner_of == owner, 1.0, 0.0)
        before = lax.dot_general(hit.astype(BF16), earlier, NN, preferred_element_type=F32)
        rank = jnp.sum(hit * before, axis=0, keepdims=True)
        place = CAP * owner + rank.astype(jnp.int32)
        placed[0:1, :] = place[:, :PAIRS]
        placed[1:2, :] = place[:, PAIRS:]
        asked = hit * slot.astype(F32)
        for turn in range(CAP):
            mine = jnp.where(before == float(turn), asked, 0.0).astype(BF16)
            here = jnp.where(column == CAP * sub + turn, 1.0, 0.0).astype(BF16)
            total += lax.dot_general(mine, here, NN, preferred_element_type=F32)
    wanted[...] = total.astype(jnp.int32) + NLEAF


def shards(positions, velocities, masses, time_bins, pair_owner, pair_slot, local_pairs):
    masses = masses.reshape(NLEAF, LEAF)
    bins = time_bins.reshape(NLEAF, LEAF)
    local_ids = local_pairs.transpose(0, 2, 1)
    state_shape = shape(8 * (NLEAF + 1), LEAF)
    local_shape = shape(8 * NLEAF, LEAF)
    rows_shape = shape(3 * NLEAF, LEAF)
    looked_shape = shape(4 * SLOTS, LEAF)
    pushed_shape = shape(3 * SLOTS, LEAF)
    asked_shape = shape(2 * CAP, DEVICES, dtype=jnp.int32)
    ends_shape = shape(2, PAIRS, dtype=jnp.int32)
    anywhere = pl.BlockSpec(memory_space=pl.ANY)
    dma = pltpu.SemaphoreType.DMA
    asked_scratch = [pltpu.SMEM((2 * CAP, DEVICES), jnp.int32), dma(())]

    def local_forces(ids, state):
        return call(local_kernel, local_shape, [state], 64 * 2**14 * 25, 2**20, scalars=[ids])

    def remote_forces(places, arrived):
        scratch = [pltpu.SMEM((2, PAIRS), jnp.int32), dma(())]
        return call(
            remote_kernel, pushed_shape, [places, arrived], 128 * 2**14 * 25, 2**21, scratch
        )

    *placed, wanted = call(
        request_kernel,
        (ends_shape, ends_shape, shape(DEVICES, LEAF, dtype=jnp.int32)),
        [pair_owner.transpose(0, 2, 1), pair_slot.transpose(0, 2, 1)],
        2**26,
        2**18,
        [pltpu.VMEM((2, 2, PAIRS), jnp.int32), pltpu.VMEM((2, 2, PAIRS), jnp.int32), dma((2,))],
        [pl.BlockSpec(memory_space=pltpu.HBM)] * 2,
    )
    wanted = exchange(wanted.reshape(DEVICES, 1, LEAF)).reshape(DEVICES, LEAF)
    state, where, moving = call(
        pack_kernel,
        (state_shape, rows_shape, rows_shape),
        [positions, velocities, masses],
        2**16,
        2**20,
    )
    local = local_forces(local_ids[0], state)
    looked, asked = call(
        gather_kernel,
        (looked_shape, asked_shape),
        [wanted, state, local],
        2**16,
        2**21,
        asked_scratch,
        [VMEM, VMEM, anywhere],
    )
    pushed = remote_forces(placed[0], send_leaves(looked))
    returned = send_forces(pushed)
    looked, state, where, moving = call(
        advance_kernel,
        (looked_shape, state_shape, rows_shape, rows_shape),
        [asked, returned, local, masses, where, moving, bins],
        2**16,
        2**22,
        asked_scratch,
    )
    local = local_forces(local_ids[1], state)
    pushed = remote_forces(placed[1], send_leaves(looked))
    returned = send_forces(pushed)
    out = shape(3, NLEAF * LEAF)
    return call(
        finish_kernel,
        (out, out, out),
        [asked, returned, local, where, moving, bins],
        2**16,
        2**22,
        [pltpu.VMEM((3, 3 * NLEAF, LEAF), F32)],
    )


def solution(mesh):
    split = P(None, AXES)
    rows = P(None, AXES, None)
    return jax.shard_map(
        shards,
        mesh=mesh,
        in_specs=(split, split, P(AXES), P(AXES), rows, rows, rows),
        out_specs=(split, split, split),
        check_vma=False,
    )
```

```python
import functools

import jax
import jax.numpy as jnp
from jax import lax
from jax.experimental import pallas as pl
from jax.experimental.pallas import tpu as pltpu
from jax.sharding import PartitionSpec as P

LEAF = 128
NLEAF = 64
DEVICES = 128
CAP = 4
PAIRS = 128
LOCAL = 64
SLOTS = DEVICES * CAP
AXES = ("gx", "gy", "gz")

SOFTENING = 0.01
CUTOFF_SQ = 0.04
TIME_STEP = 0.05
CENTRE = 0.5

F32 = jnp.float32
BF16 = jnp.bfloat16
NT = (((1,), (1,)), ((), ()))
NN = (((1,), (0,)), ((), ()))
TN = (((0,), (0,)), ((), ()))
VMEM = pl.BlockSpec(memory_space=pltpu.VMEM)


def split3(value):
    high = value.astype(BF16).astype(F32)
    rest = value - high
    middle = rest.astype(BF16).astype(F32)
    return high, middle, rest - middle


def pair_parts(tile, row):
    vector = (row & 3) < 3
    xyz = jnp.where(vector, tile - CENTRE, 0.0)
    parts = split3(xyz)
    square = xyz * xyz
    norm = pltpu.roll(square, 1, 0) + pltpu.roll(square, 2, 0) + pltpu.roll(square, 3, 0)
    norms = split3(norm + jnp.where(row == 3, SOFTENING, 0.0))
    mass = jnp.where(row < 4, tile[3:4], tile[7:8]) * (1.0 / CUTOFF_SQ**2)
    weights = split3(jnp.where(vector, xyz, 1.0) * mass)
    weights = jnp.concatenate([*weights, jnp.zeros_like(xyz)], axis=0).astype(BF16)
    return xyz, parts, norms, weights


def softened_distances(parts, norms, row):
    high, middle, low = parts
    minus_two = jnp.where(row < 3, -2.0, 0.0)
    h2, m2, l2 = (pltpu.roll(part, 4, 0) * minus_two for part in parts)
    lhs, rhs = [], []
    for left, right, norm in zip(parts, (h2, h2, h2), norms):
        lhs.append(left + jnp.where(row == 3, norm, jnp.where(row == 7, 1.0, 0.0)))
        rhs.append(right + jnp.where(row == 7, norm, jnp.where(row == 3, 1.0, 0.0)))
    lhs = jnp.concatenate(lhs + [high, high, middle], axis=0).astype(BF16)
    rhs = jnp.concatenate(rhs + [m2, l2, m2], axis=0).astype(BF16)
    return lax.dot_general(lhs, rhs, TN, preferred_element_type=F32)


def pair_kernel(softened):
    taper = jnp.maximum((CUTOFF_SQ + SOFTENING) - softened, 0.0)
    root = lax.rsqrt(softened)
    scaled = taper * root
    kernel = scaled * scaled * root
    high = kernel.astype(BF16)
    return high, (kernel - high.astype(F32)).astype(BF16)


def moments(weights, kernel):
    high, low = kernel
    twice = jnp.concatenate([weights, weights], axis=1)
    on_left = lax.dot_general(
        jnp.concatenate([high, low], axis=1), twice, NT, preferred_element_type=F32
    ).T
    on_right = lax.dot_general(
        twice, jnp.concatenate([high, low], axis=0), NN, preferred_element_type=F32
    )
    return on_left, on_right


def force_tile(sums, xyz, row):
    on_left, on_right = (part[0:8] + part[8:16] + part[16:24] for part in sums)
    total = jnp.where(row < 4, on_right, on_left)
    mass = jnp.where(row < 4, total[3:4], total[7:8])
    return total - pltpu.roll(xyz, 4, 0) * mass


def pair_forces(tiles, row):
    count = len(tiles)
    parts, dists, sums, out = {}, {}, {}, []
    for step in range(count + 10):
        if step < count:
            parts[step] = pair_parts(tiles[step], row)
            dists[step] = softened_distances(parts[step][1], parts[step][2], row)
        k = step - 6
        if 0 <= k < count:
            sums[k] = moments(parts[k][3], pair_kernel(dists[k]))
        k = step - 10
        if k >= 0:
            out.append(force_tile(sums[k], parts[k][0], row))
    return out


def row_iota():
    return lax.broadcasted_iota(jnp.int32, (8, LEAF), 0)


def leaf_tile(state, leaf):
    return state[pl.ds(pl.multiple_of(leaf * 8, 8), 8), :]


def fill_slots(first, wanted, leaves, looked):
    parts = jnp.concatenate([part.astype(BF16) for part in split3(leaves)], axis=0)
    leaf = lax.broadcasted_iota(jnp.int32, (DEVICES, 3 * NLEAF), 1) & (NLEAF - 1)
    for turn in range(CAP):
        chosen = jnp.where(leaf == wanted[:, first + turn : first + turn + 1], 1.0, 0.0)
        found = lax.dot_general(chosen.astype(BF16), parts, NN, preferred_element_type=F32)
        for index in range(4):
            looked[pl.ds(4 * turn + index, DEVICES, stride=4 * CAP), :] = found[
                :, index * LEAF : (index + 1) * LEAF
            ]


def component(index):
    return slice(index * NLEAF, (index + 1) * NLEAF)


def store_state(state, index, value):
    state[pl.ds(index, NLEAF, stride=8), :] = value
    state[pl.ds(index + 4, NLEAF, stride=8), :] = value


def pack_kernel(positions, velocities, masses, places0, places1, state, where, moving, placed0, placed1):
    placed0[...] = places0[...]
    placed1[...] = places1[...]
    for leaf in range(NLEAF):
        lanes = slice(leaf * LEAF, (leaf + 1) * LEAF)
        where[pl.ds(leaf, 3, stride=NLEAF), :] = positions[:, lanes]
        moving[pl.ds(leaf, 3, stride=NLEAF), :] = velocities[:, lanes]
    for index in range(3):
        store_state(state, index, where[component(index), :])
    store_state(state, 3, masses[...])


def gather_kernel(wanted, where, masses, _, looked, asked):
    asked[...] = wanted[...].T[: 2 * CAP]
    leaves = [where[component(index), :] for index in range(3)] + [masses[...]]
    fill_slots(0, wanted, jnp.concatenate(leaves, axis=1), looked)


def local_kernel(pairs, state, forces):
    row = row_iota()
    forces[...] = jnp.zeros_like(forces)
    unroll = 32

    def body(step, carry):
        ids = [
            (pairs[0, step * unroll + u], pairs[1, step * unroll + u])
            for u in range(unroll)
        ]
        found = pair_forces([jnp.where(row < 4, leaf_tile(state, a), leaf_tile(state, b)) for a, b in ids], row)
        for (a, b), force in zip(ids, found):
            to_left = pl.ds(pl.multiple_of(a * 8, 8), 8)
            to_right = pl.ds(pl.multiple_of(b * 8, 8), 8)
            forces[to_left, :] += jnp.where(row < 4, 0.0, force)
            forces[to_right, :] += jnp.where(row < 4, force, 0.0)
        return carry

    lax.fori_loop(0, LOCAL // unroll, body, 0)


def remote_kernel(unused, places, arrived, *refs):
    pushed, placed, sem = refs[unused:]
    row = row_iota()
    copy = pltpu.make_async_copy(places, placed, sem)
    copy.start()
    pushed[...] = jnp.zeros_like(pushed)
    copy.wait()
    unroll = 64

    def leaf(slot, half):
        tile = arrived[pl.ds(pl.multiple_of((slot >> 1) * 8, 8), 8), :]
        return jnp.where((slot & 1) == half, tile, pltpu.roll(tile, 4, 0))

    def body(step, carry):
        ids = [
            (placed[0, step * unroll + u], placed[1, step * unroll + u])
            for u in range(unroll)
        ]
        found = pair_forces([jnp.where(row < 4, leaf(a, 0), leaf(b, 1)) for a, b in ids], row)
        for (a, b), force in zip(ids, found):
            pushed[pl.ds(3 * a, 3), :] = force[4:7]
            pushed[pl.ds(3 * b, 3), :] = force[0:3]
        return carry

    lax.fori_loop(0, PAIRS // unroll, body, 0)


def summed(first, asked, returned):
    target = lax.broadcasted_iota(jnp.int32, (NLEAF, DEVICES), 0)
    chosen, blocks = [], []
    for turn in range(CAP):
        chosen.append(jnp.where(target == asked[first + turn : first + turn + 1, :], 1.0, 0.0))
        rows = [
            returned[pl.ds(3 * turn + index, DEVICES, stride=3 * CAP), :] for index in range(3)
        ]
        blocks.append(jnp.concatenate(rows, axis=1))
    chosen = jnp.concatenate(chosen, axis=1).astype(BF16)
    total = jnp.zeros((NLEAF, 3 * LEAF), F32)
    for part in split3(jnp.concatenate(blocks, axis=0)):
        total += lax.dot_general(chosen, part.astype(BF16), NN, preferred_element_type=F32)
    return total


def kick_drift(subcycle, asked, returned, local, where, moving, bins):
    total = summed(CAP * subcycle, asked, returned)
    active = bins[...] >= 3 - subcycle
    for index in range(3):
        accel = total[:, index * LEAF : (index + 1) * LEAF]
        accel += local[pl.ds(index, NLEAF, stride=8), :] + local[pl.ds(index + 4, NLEAF, stride=8), :]
        velocity = moving[component(index), :] + jnp.where(active, TIME_STEP * accel, 0.0)
        yield index, accel, velocity, where[component(index), :] + TIME_STEP * velocity


def advance_kernel(
    wanted, asked, returned, local, masses, where, moving, bins, looked, state, new_where, new_moving
):
    leaves = []
    for index, _, velocity, position in kick_drift(0, asked, returned, local, where, moving, bins):
        new_moving[component(index), :] = velocity
        new_where[component(index), :] = position
        store_state(state, index, position)
        leaves.append(position)
    leaves.append(masses[...])
    fill_slots(CAP, wanted, jnp.concatenate(leaves, axis=1), looked)
    store_state(state, 3, masses[...])


def finish_kernel(asked, returned, local, where, moving, bins, positions, velocities, accels, rows):
    for index, *results in kick_drift(1, asked, returned, local, where, moving, bins):
        for number, result in enumerate(results):
            rows[number, component(index), :] = result
    for leaf in range(NLEAF):
        lanes = slice(leaf * LEAF, (leaf + 1) * LEAF)
        for number, out in enumerate((accels, velocities, positions)):
            out[:, lanes] = rows[number, pl.ds(leaf, 3, stride=NLEAF), :]


def call(
    kernel, out_shapes, arrays, flops, size, scratch=(), in_specs=None, scalars=(), vmem=40 * 2**20
):
    return pl.pallas_call(
        kernel,
        out_shape=out_shapes,
        grid_spec=pltpu.PrefetchScalarGridSpec(
            num_scalar_prefetch=len(scalars),
            grid=(),
            in_specs=in_specs or [VMEM] * len(arrays),
            out_specs=jax.tree.map(lambda _: VMEM, out_shapes),
            scratch_shapes=scratch,
        ),
        compiler_params=pltpu.CompilerParams(vmem_limit_bytes=vmem),
        cost_estimate=pl.CostEstimate(flops=flops, bytes_accessed=size, transcendentals=0),
    )(*scalars, *arrays)


def shape(*dims, dtype=F32):
    return jax.ShapeDtypeStruct(dims, dtype)


def exchange(array):
    return lax.all_to_all(array, AXES, split_axis=0, concat_axis=0, tiled=True)


def send_leaves(looked):
    return exchange(looked.reshape(DEVICES, 4 * CAP, LEAF)).reshape(4 * SLOTS, LEAF)


def send_forces(pushed):
    return exchange(pushed.reshape(DEVICES, 3, CAP, LEAF)).reshape(3 * SLOTS, LEAF)


def request_kernel(pair_owner, pair_slot, placed0, placed1, wanted, owners, slots, sems):
    copies = [
        pltpu.make_async_copy(pair_owner, owners, sems.at[0]),
        pltpu.make_async_copy(pair_slot, slots, sems.at[1]),
    ]
    for copy in copies:
        copy.start()
    for copy in copies:
        copy.wait()
    ends = 2 * PAIRS
    owner_of = lax.broadcasted_iota(jnp.int32, (DEVICES, ends), 0)
    earlier = lax.broadcasted_iota(jnp.int32, (ends, ends), 0) < lax.broadcasted_iota(
        jnp.int32, (ends, ends), 1
    )
    earlier = jnp.where(earlier, 1.0, 0.0).astype(BF16)
    column = lax.broadcasted_iota(jnp.int32, (ends, LEAF), 1)
    total = jnp.zeros((DEVICES, LEAF), F32)
    for sub, placed in enumerate((placed0, placed1)):
        owner = jnp.concatenate([owners[sub, 0:1], owners[sub, 1:2]], axis=1)
        slot = jnp.concatenate([slots[sub, 0:1], slots[sub, 1:2]], axis=1) - NLEAF
        hit = jnp.where(owner_of == owner, 1.0, 0.0)
        before = lax.dot_general(hit.astype(BF16), earlier, NN, preferred_element_type=F32)
        rank = jnp.sum(hit * before, axis=0, keepdims=True)
        place = CAP * owner + rank.astype(jnp.int32)
        placed[0:1, :] = place[:, :PAIRS]
        placed[1:2, :] = place[:, PAIRS:]
        asked = hit * slot.astype(F32)
        for turn in range(CAP):
            mine = jnp.where(before == float(turn), asked, 0.0).astype(BF16)
            here = jnp.where(column == CAP * sub + turn, 1.0, 0.0).astype(BF16)
            total += lax.dot_general(mine, here, NN, preferred_element_type=F32)
    wanted[...] = total.astype(jnp.int32) + NLEAF


def shards(positions, velocities, masses, time_bins, pair_owner, pair_slot, local_pairs):
    masses = masses.reshape(NLEAF, LEAF)
    bins = time_bins.reshape(NLEAF, LEAF)
    local_ids = local_pairs.transpose(0, 2, 1)
    tiles_shape = shape(8 * NLEAF, LEAF)
    rows_shape = shape(3 * NLEAF, LEAF)
    looked_shape = shape(4 * SLOTS, LEAF)
    pushed_shape = shape(3 * SLOTS, LEAF)
    asked_shape = shape(2 * CAP, DEVICES, dtype=jnp.int32)
    ends_shape = shape(2, PAIRS, dtype=jnp.int32)
    anywhere = pl.BlockSpec(memory_space=pl.ANY)
    dma = pltpu.SemaphoreType.DMA

    def local_forces(ids, state):
        return call(local_kernel, tiles_shape, [state], 64 * 2**14 * 25, 2**20, scalars=[ids])

    def remote_forces(places, arrived, *earlier):
        scratch = [pltpu.SMEM((2, PAIRS), jnp.int32), dma(())]
        specs = [VMEM] * 2 + [anywhere] * len(earlier)
        return call(
            functools.partial(remote_kernel, len(earlier)),
            pushed_shape,
            [places, arrived, *earlier],
            128 * 2**14 * 25,
            2**21,
            scratch,
            specs,
        )

    *placed, wanted = call(
        request_kernel,
        (ends_shape, ends_shape, shape(DEVICES, LEAF, dtype=jnp.int32)),
        [pair_owner.transpose(0, 2, 1), pair_slot.transpose(0, 2, 1)],
        2**26,
        2**18,
        [pltpu.VMEM((2, 2, PAIRS), jnp.int32), pltpu.VMEM((2, 2, PAIRS), jnp.int32), dma((2,))],
        [pl.BlockSpec(memory_space=pltpu.HBM)] * 2,
        vmem=60 * 2**20,
    )
    wanted = exchange(wanted.reshape(DEVICES, 1, LEAF)).reshape(DEVICES, LEAF)
    state, where, moving, *placed = call(
        pack_kernel,
        (tiles_shape, rows_shape, rows_shape, ends_shape, ends_shape),
        [positions, velocities, masses, *placed],
        2**16,
        2**20,
    )
    local = local_forces(local_ids[0], state)
    looked, asked = call(
        gather_kernel,
        (looked_shape, asked_shape),
        [wanted, where, masses, local],
        2**16,
        2**21,
        in_specs=[VMEM, VMEM, VMEM, anywhere],
    )
    pushed = remote_forces(placed[0], send_leaves(looked))
    returned = send_forces(pushed)
    looked, state, where, moving = call(
        advance_kernel,
        (looked_shape, tiles_shape, rows_shape, rows_shape),
        [wanted, asked, returned, local, masses, where, moving, bins],
        2**16,
        2**22,
    )
    local = local_forces(local_ids[1], state)
    pushed = remote_forces(placed[1], send_leaves(looked), local)
    returned = send_forces(pushed)
    out = shape(3, NLEAF * LEAF)
    return call(
        finish_kernel,
        (out, out, out),
        [asked, returned, local, where, moving, bins],
        2**16,
        2**22,
        [pltpu.VMEM((3, 3 * NLEAF, LEAF), F32)],
    )


def solution(mesh):
    split = P(None, AXES)
    rows = P(None, AXES, None)
    return jax.shard_map(
        shards,
        mesh=mesh,
        in_specs=(split, split, P(AXES), P(AXES), rows, rows, rows),
        out_specs=(split, split, split),
        check_vma=False,
    )
```

```python
import functools

import jax
import jax.numpy as jnp
from jax import lax
from jax.experimental import pallas as pl
from jax.experimental.pallas import tpu as pltpu
from jax.sharding import PartitionSpec as P

LEAF = 128
NLEAF = 64
DEVICES = 128
CAP = 4
PAIRS = 128
LOCAL = 64
SLOTS = DEVICES * CAP
AXES = ("gx", "gy", "gz")

SOFTENING = 0.01
CUTOFF_SQ = 0.04
TIME_STEP = 0.05
CENTRE = 0.5

F32 = jnp.float32
BF16 = jnp.bfloat16
NT = (((1,), (1,)), ((), ()))
NN = (((1,), (0,)), ((), ()))
TN = (((0,), (0,)), ((), ()))
VMEM = pl.BlockSpec(memory_space=pltpu.VMEM)


def split3(value):
    high = value.astype(BF16).astype(F32)
    rest = value - high
    middle = rest.astype(BF16).astype(F32)
    return high, middle, rest - middle


def pair_parts(tile, row):
    vector = (row & 3) < 3
    xyz = jnp.where(vector, tile - CENTRE, 0.0)
    parts = split3(xyz)
    square = xyz * xyz
    norm = pltpu.roll(square, 1, 0) + pltpu.roll(square, 2, 0) + pltpu.roll(square, 3, 0)
    norms = split3(norm + jnp.where(row == 3, SOFTENING, 0.0))
    mass = jnp.where(row < 4, tile[3:4], tile[7:8]) * (1.0 / CUTOFF_SQ**2)
    weights = split3(jnp.where(vector, xyz, 1.0) * mass)
    weights = jnp.concatenate([*weights, jnp.zeros_like(xyz)], axis=0).astype(BF16)
    return xyz, parts, norms, weights


def softened_distances(parts, norms, row):
    high, middle, low = parts
    minus_two = jnp.where(row < 3, -2.0, 0.0)
    h2, m2, l2 = (pltpu.roll(part, 4, 0) * minus_two for part in parts)
    lhs, rhs = [], []
    for left, right, norm in zip(parts, (h2, h2, h2), norms):
        lhs.append(left + jnp.where(row == 3, norm, jnp.where(row == 7, 1.0, 0.0)))
        rhs.append(right + jnp.where(row == 7, norm, jnp.where(row == 3, 1.0, 0.0)))
    lhs = jnp.concatenate(lhs + [high, high, middle], axis=0).astype(BF16)
    rhs = jnp.concatenate(rhs + [m2, l2, m2], axis=0).astype(BF16)
    return lax.dot_general(lhs, rhs, TN, preferred_element_type=F32)


def pair_kernel(softened):
    taper = jnp.maximum((CUTOFF_SQ + SOFTENING) - softened, 0.0)
    root = lax.rsqrt(softened)
    scaled = taper * root
    kernel = scaled * scaled * root
    high = kernel.astype(BF16)
    return high, (kernel - high.astype(F32)).astype(BF16)


def moments(weights, kernel):
    high, low = kernel
    twice = jnp.concatenate([weights, weights], axis=1)
    on_left = lax.dot_general(
        jnp.concatenate([high, low], axis=1), twice, NT, preferred_element_type=F32
    ).T
    on_right = lax.dot_general(
        twice, jnp.concatenate([high, low], axis=0), NN, preferred_element_type=F32
    )
    return on_left, on_right


def force_tile(sums, xyz, row):
    on_left, on_right = (part[0:8] + part[8:16] + part[16:24] for part in sums)
    total = jnp.where(row < 4, on_right, on_left)
    mass = jnp.where(row < 4, total[3:4], total[7:8])
    return total - pltpu.roll(xyz, 4, 0) * mass


def pair_forces(tiles, row):
    count = len(tiles)
    parts, dists, sums, out = {}, {}, {}, []
    for step in range(count + 10):
        if step < count:
            parts[step] = pair_parts(tiles[step], row)
            dists[step] = softened_distances(parts[step][1], parts[step][2], row)
        k = step - 6
        if 0 <= k < count:
            sums[k] = moments(parts[k][3], pair_kernel(dists[k]))
        k = step - 10
        if k >= 0:
            out.append(force_tile(sums[k], parts[k][0], row))
    return out


def row_iota():
    return lax.broadcasted_iota(jnp.int32, (8, LEAF), 0)


def leaf_tile(state, leaf):
    return state[pl.ds(pl.multiple_of(leaf * 8, 8), 8), :]


def fill_slots(first, wanted, leaves, looked):
    parts = jnp.concatenate([part.astype(BF16) for part in split3(leaves)], axis=0)
    leaf = lax.broadcasted_iota(jnp.int32, (DEVICES, 3 * NLEAF), 1) & (NLEAF - 1)
    for turn in range(CAP):
        chosen = jnp.where(leaf == wanted[:, first + turn : first + turn + 1], 1.0, 0.0)
        found = lax.dot_general(chosen.astype(BF16), parts, NN, preferred_element_type=F32)
        for index in range(4):
            looked[pl.ds(4 * turn + index, DEVICES, stride=4 * CAP), :] = found[
                :, index * LEAF : (index + 1) * LEAF
            ]


def component(index):
    return slice(index * NLEAF, (index + 1) * NLEAF)


def store_state(state, index, value):
    state[pl.ds(index, NLEAF, stride=8), :] = value
    state[pl.ds(index + 4, NLEAF, stride=8), :] = value


def pack_kernel(
    positions, velocities, masses, bins, places0, places1,
    state, where, moving, placed0, placed1, order, ordered,
):
    placed0[...] = places0[...]
    placed1[...] = places1[...]
    for leaf in range(NLEAF):
        lanes = slice(leaf * LEAF, (leaf + 1) * LEAF)
        where[pl.ds(leaf, 3, stride=NLEAF), :] = positions[:, lanes]
        moving[pl.ds(leaf, 3, stride=NLEAF), :] = velocities[:, lanes]
    for index in range(3):
        store_state(state, index, where[component(index), :])
    store_state(state, 3, masses[...])
    kicked = jnp.where(bins[...] >= 3, 1.0, 0.0)
    earlier = lax.broadcasted_iota(jnp.int32, (LEAF, LEAF), 0) < lax.broadcasted_iota(
        jnp.int32, (LEAF, LEAF), 1
    )
    before = lax.dot_general(
        kicked.astype(BF16), jnp.where(earlier, 1.0, 0.0).astype(BF16), NN, preferred_element_type=F32
    )
    lane = lax.broadcasted_iota(jnp.int32, (NLEAF, LEAF), 1).astype(F32)
    last = jnp.sum(kicked, axis=1, keepdims=True) + lane - before
    order[...] = jnp.where(kicked > 0.0, before, last).astype(jnp.int32)

    def body(step, carry):
        for u in range(8):
            leaf = step * 8 + u
            moved = lax.dot_general(
                stacked(split3(leaf_tile(state, leaf))), lanes_of(order, leaf, LEAF), NT,
                preferred_element_type=F32,
            )
            ordered[pl.ds(pl.multiple_of(leaf * 8, 8), 8), :] = moved[0:8] + moved[8:16] + moved[16:24]
        return carry

    lax.fori_loop(0, NLEAF // 8, body, 0)


def stacked(parts):
    return jnp.concatenate([*parts, jnp.zeros_like(parts[0])], axis=0).astype(BF16)


def lanes_of(order, leaf, count):
    lane = lax.broadcasted_iota(jnp.int32, (count, LEAF), 0)
    return jnp.where(lane == order[pl.ds(leaf, 1), :], 1.0, 0.0).astype(BF16)


def gather_kernel(wanted, ordered, looked, asked, most):
    asked[...] = wanted[...].T[: 2 * CAP]
    most[...] = jnp.max(wanted[:, 2 * CAP : 2 * CAP + 1], axis=0, keepdims=True)
    leaves = [ordered[pl.ds(index, NLEAF, stride=8), :] for index in range(4)]
    fill_slots(0, wanted, jnp.concatenate(leaves, axis=1), looked)


def local_kernel(pairs, state, forces):
    row = row_iota()
    forces[...] = jnp.zeros_like(forces)
    unroll = 32

    def body(step, carry):
        ids = [
            (pairs[0, step * unroll + u], pairs[1, step * unroll + u])
            for u in range(unroll)
        ]
        found = pair_forces([jnp.where(row < 4, leaf_tile(state, a), leaf_tile(state, b)) for a, b in ids], row)
        for (a, b), force in zip(ids, found):
            to_left = pl.ds(pl.multiple_of(a * 8, 8), 8)
            to_right = pl.ds(pl.multiple_of(b * 8, 8), 8)
            forces[to_left, :] += jnp.where(row < 4, 0.0, force)
            forces[to_right, :] += jnp.where(row < 4, force, 0.0)
        return carry

    lax.fori_loop(0, LOCAL // unroll, body, 0)


def remote_kernel(unused, half, places, arrived, *refs):
    pushed, placed, sem, *apart = refs[unused:]
    forces = apart[0] if half else pushed
    row = row_iota()
    copy = pltpu.make_async_copy(places, placed, sem)
    copy.start()
    forces[...] = jnp.zeros_like(forces)
    copy.wait()
    unroll = 64

    def leaf(slot, half):
        tile = arrived[pl.ds(pl.multiple_of((slot >> 1) * 8, 8), 8), :]
        return jnp.where((slot & 1) == half, tile, pltpu.roll(tile, 4, 0))

    def body(step, carry):
        ids = [
            (placed[0, step * unroll + u], placed[1, step * unroll + u])
            for u in range(unroll)
        ]
        found = pair_forces([jnp.where(row < 4, leaf(a, 0), leaf(b, 1)) for a, b in ids], row)
        for (a, b), force in zip(ids, found):
            for slot, first in ((a, 4), (b, 0)):
                at = 3 * ((slot >> 1) + (slot & 1) * (SLOTS // 2)) if half else 3 * slot
                forces[pl.ds(at, 3), :] = force[first : first + 3]
        return carry

    lax.fori_loop(0, PAIRS // unroll, body, 0)
    if half:
        rows = pushed.shape[0]
        lower = lax.broadcasted_iota(jnp.int32, (rows, LEAF), 1) < LEAF // 2
        odd = pltpu.roll(forces[rows:, :], LEAF // 2, 1)
        pushed[...] = jnp.where(lower, forces[:rows, :], odd)


def summed(first, half, asked, returned):
    target = lax.broadcasted_iota(jnp.int32, (NLEAF, DEVICES), 0)
    chosen = [
        jnp.where(target == asked[first + turn : first + turn + 1, :], 1.0, 0.0) for turn in range(CAP)
    ]
    groups = CAP // 2 if half else CAP
    blocks = [
        jnp.concatenate(
            [returned[pl.ds(3 * group + index, DEVICES, stride=3 * groups), :] for index in range(3)],
            axis=1,
        )
        for group in range(groups)
    ]
    if half:
        even, odd = (jnp.concatenate(chosen[part::2], axis=1) for part in range(2))
        chosen = jnp.concatenate([even, odd], axis=0).astype(BF16)
    else:
        chosen = jnp.concatenate(chosen, axis=1).astype(BF16)
    total = jnp.zeros((chosen.shape[0], 3 * LEAF), F32)
    for part in split3(jnp.concatenate(blocks, axis=0)):
        total += lax.dot_general(chosen, part.astype(BF16), NN, preferred_element_type=F32)
    totals = [total[:, index * LEAF : (index + 1) * LEAF] for index in range(3)]
    if half:
        lower = lax.broadcasted_iota(jnp.int32, (NLEAF, LEAF), 1) < LEAF // 2
        totals = [
            jnp.where(lower, one[:NLEAF] + pltpu.roll(one[NLEAF:], LEAF // 2, 1), 0.0) for one in totals
        ]
    return totals


def disordered(totals, half, order, rows, spread):
    rows[...] = jnp.zeros_like(rows)
    for index, total in enumerate(totals):
        for number, part in enumerate(split3(total)):
            rows[number, component(index), :] = part
    count = LEAF // 2 if half else LEAF

    def body(step, carry):
        for u in range(32):
            leaf = step * 32 + u
            parts = [rows[number, pl.ds(leaf, 8, stride=NLEAF), :] for number in range(3)]
            moved = lax.dot_general(
                stacked(parts)[:, :count], lanes_of(order, leaf, count), NN, preferred_element_type=F32
            )
            moved = moved[0:8] + moved[8:16] + moved[16:24]
            spread[pl.ds(leaf, 3, stride=NLEAF), :] = moved[0:3]
        return carry

    lax.fori_loop(0, NLEAF // 32, body, 0)
    return [spread[component(index), :] for index in range(3)]


def kick_drift(threshold, totals, local, where, moving, bins):
    active = bins[...] >= threshold
    for index, accel in enumerate(totals):
        accel += local[pl.ds(index, NLEAF, stride=8), :] + local[pl.ds(index + 4, NLEAF, stride=8), :]
        velocity = moving[component(index), :] + jnp.where(active, TIME_STEP * accel, 0.0)
        yield index, accel, velocity, where[component(index), :] + TIME_STEP * velocity


def advance_kernel(
    half, wanted, asked, returned, local, masses, where, moving, bins, order,
    looked, state, new_where, new_moving, rows, spread,
):
    totals = disordered(summed(0, half, asked, returned), half, order, rows, spread)
    leaves = []
    for index, _, velocity, position in kick_drift(3, totals, local, where, moving, bins):
        new_moving[component(index), :] = velocity
        new_where[component(index), :] = position
        store_state(state, index, position)
        leaves.append(position)
    leaves.append(masses[...])
    fill_slots(CAP, wanted, jnp.concatenate(leaves, axis=1), looked)
    store_state(state, 3, masses[...])


def finish_kernel(asked, returned, local, where, moving, bins, positions, velocities, accels, rows):
    totals = summed(CAP, False, asked, returned)
    for index, *results in kick_drift(2, totals, local, where, moving, bins):
        for number, result in enumerate(results):
            rows[number, component(index), :] = result
    for leaf in range(NLEAF):
        lanes = slice(leaf * LEAF, (leaf + 1) * LEAF)
        for number, out in enumerate((accels, velocities, positions)):
            out[:, lanes] = rows[number, pl.ds(leaf, 3, stride=NLEAF), :]


def call(
    kernel, out_shapes, arrays, flops, size, scratch=(), in_specs=None, scalars=(), vmem=40 * 2**20
):
    return pl.pallas_call(
        kernel,
        out_shape=out_shapes,
        grid_spec=pltpu.PrefetchScalarGridSpec(
            num_scalar_prefetch=len(scalars),
            grid=(),
            in_specs=in_specs or [VMEM] * len(arrays),
            out_specs=jax.tree.map(lambda _: VMEM, out_shapes),
            scratch_shapes=scratch,
        ),
        compiler_params=pltpu.CompilerParams(vmem_limit_bytes=vmem),
        cost_estimate=pl.CostEstimate(flops=flops, bytes_accessed=size, transcendentals=0),
    )(*scalars, *arrays)


def shape(*dims, dtype=F32):
    return jax.ShapeDtypeStruct(dims, dtype)


def exchange(array):
    return lax.all_to_all(array, AXES, split_axis=0, concat_axis=0, tiled=True)


def send_leaves(looked):
    return exchange(looked.reshape(DEVICES, 4 * CAP, LEAF)).reshape(4 * SLOTS, LEAF)


def send_forces(pushed):
    return exchange(pushed.reshape(DEVICES, 3, -1, LEAF)).reshape(pushed.shape)


def request_kernel(pair_owner, pair_slot, time_bins, placed0, placed1, wanted, owners, slots, bins, sems):
    copies = [
        pltpu.make_async_copy(time_bins, bins, sems.at[2]),
        pltpu.make_async_copy(pair_owner, owners, sems.at[0]),
        pltpu.make_async_copy(pair_slot, slots, sems.at[1]),
    ]
    for copy in copies:
        copy.start()
    for copy in copies:
        copy.wait()
    ends = 2 * PAIRS
    owner_of = lax.broadcasted_iota(jnp.int32, (DEVICES, ends), 0)
    earlier = lax.broadcasted_iota(jnp.int32, (ends, ends), 0) < lax.broadcasted_iota(
        jnp.int32, (ends, ends), 1
    )
    earlier = jnp.where(earlier, 1.0, 0.0).astype(BF16)
    column = lax.broadcasted_iota(jnp.int32, (ends, LEAF), 1)
    total = jnp.zeros((DEVICES, LEAF), F32)
    for sub, placed in enumerate((placed0, placed1)):
        owner = jnp.concatenate([owners[sub, 0:1], owners[sub, 1:2]], axis=1)
        slot = jnp.concatenate([slots[sub, 0:1], slots[sub, 1:2]], axis=1) - NLEAF
        hit = jnp.where(owner_of == owner, 1.0, 0.0)
        before = lax.dot_general(hit.astype(BF16), earlier, NN, preferred_element_type=F32)
        rank = jnp.sum(hit * before, axis=0, keepdims=True)
        place = CAP * owner + rank.astype(jnp.int32)
        placed[0:1, :] = place[:, :PAIRS]
        placed[1:2, :] = place[:, PAIRS:]
        asked = hit * slot.astype(F32)
        for turn in range(CAP):
            mine = jnp.where(before == float(turn), asked, 0.0).astype(BF16)
            here = jnp.where(column == CAP * sub + turn, 1.0, 0.0).astype(BF16)
            total += lax.dot_general(mine, here, NN, preferred_element_type=F32)
    kicked = jnp.sum(jnp.where(bins[...] >= 3, 1.0, 0.0), axis=1, keepdims=True)
    most = jnp.max(kicked, axis=0, keepdims=True)
    lane = lax.broadcasted_iota(jnp.int32, (DEVICES, LEAF), 1)
    wanted[...] = jnp.where(lane == 2 * CAP, most, total + float(NLEAF)).astype(jnp.int32)


def shards(positions, velocities, masses, time_bins, pair_owner, pair_slot, local_pairs):
    masses = masses.reshape(NLEAF, LEAF)
    bins = time_bins.reshape(NLEAF, LEAF)
    local_ids = local_pairs.transpose(0, 2, 1)
    tiles_shape = shape(8 * NLEAF, LEAF)
    rows_shape = shape(3 * NLEAF, LEAF)
    looked_shape = shape(4 * SLOTS, LEAF)
    asked_shape = shape(2 * CAP, DEVICES, dtype=jnp.int32)
    ends_shape = shape(2, PAIRS, dtype=jnp.int32)
    anywhere = pl.BlockSpec(memory_space=pl.ANY)
    dma = pltpu.SemaphoreType.DMA

    def local_forces(ids, state):
        return call(local_kernel, tiles_shape, [state], 64 * 2**14 * 25, 2**20, scalars=[ids])

    def remote_forces(places, arrived, *earlier, half=False):
        scratch = [pltpu.SMEM((2, PAIRS), jnp.int32), dma(())]
        if half:
            scratch.append(pltpu.VMEM((3 * SLOTS, LEAF), F32))
        specs = [VMEM] * 2 + [anywhere] * len(earlier)
        return call(
            functools.partial(remote_kernel, len(earlier), half),
            shape((3 * SLOTS) // (2 if half else 1), LEAF),
            [places, arrived, *earlier],
            128 * 2**14 * 25,
            2**21,
            scratch,
            specs,
        )

    def subcycle0(half):
        def run(places, arrived, *arrays):
            returned = send_forces(remote_forces(places, arrived, half=half))
            wanted, asked, *others = arrays
            return call(
                functools.partial(advance_kernel, half),
                (looked_shape, tiles_shape, rows_shape, rows_shape),
                [wanted, asked, returned, *others],
                2**16,
                2**22,
                [pltpu.VMEM((3, 8 * NLEAF, LEAF), F32), pltpu.VMEM((3 * NLEAF, LEAF), F32)],
            )

        return run

    *placed, wanted = call(
        request_kernel,
        (ends_shape, ends_shape, shape(DEVICES, LEAF, dtype=jnp.int32)),
        [pair_owner.transpose(0, 2, 1), pair_slot.transpose(0, 2, 1), bins],
        2**26,
        2**18,
        [
            pltpu.VMEM((2, 2, PAIRS), jnp.int32),
            pltpu.VMEM((2, 2, PAIRS), jnp.int32),
            pltpu.VMEM((NLEAF, LEAF), jnp.int32),
            dma((3,)),
        ],
        [pl.BlockSpec(memory_space=pltpu.HBM)] * 3,
        vmem=60 * 2**20,
    )
    wanted = exchange(wanted.reshape(DEVICES, 1, LEAF)).reshape(DEVICES, LEAF)
    state, where, moving, *placed, order, ordered = call(
        pack_kernel,
        (
            tiles_shape, rows_shape, rows_shape, ends_shape, ends_shape,
            shape(NLEAF, LEAF, dtype=jnp.int32), tiles_shape,
        ),
        [positions, velocities, masses, bins, *placed],
        2**16,
        2**20,
    )
    looked, asked, most = call(
        gather_kernel,
        (looked_shape, shape(2 * CAP, DEVICES, dtype=jnp.int32), shape(1, 1, dtype=jnp.int32)),
        [wanted, ordered],
        2**16,
        2**21,
    )
    local = local_forces(local_ids[0], state)
    few = most[0, 0] <= LEAF // 2
    looked, state, where, moving = lax.cond(
        few, subcycle0(True), subcycle0(False),
        placed[0], send_leaves(looked), wanted, asked, local, masses, where, moving, bins, order,
    )
    local = local_forces(local_ids[1], state)
    pushed = remote_forces(placed[1], send_leaves(looked), local)
    returned = send_forces(pushed)
    out = shape(3, NLEAF * LEAF)
    return call(
        finish_kernel,
        (out, out, out),
        [asked, returned, local, where, moving, bins],
        2**16,
        2**22,
        [pltpu.VMEM((3, 3 * NLEAF, LEAF), F32)],
    )


def solution(mesh):
    split = P(None, AXES)
    rows = P(None, AXES, None)
    return jax.shard_map(
        shards,
        mesh=mesh,
        in_specs=(split, split, P(AXES), P(AXES), rows, rows, rows),
        out_specs=(split, split, split),
        check_vma=False,
    )
```

```python
import functools

import jax
import jax.numpy as jnp
from jax import lax
from jax.experimental import pallas as pl
from jax.experimental.pallas import tpu as pltpu
from jax.sharding import PartitionSpec as P

LEAF = 128
NLEAF = 64
DEVICES = 128
CAP = 4
PAIRS = 128
LOCAL = 64
SLOTS = DEVICES * CAP
AXES = ("gx", "gy", "gz")

SOFTENING = 0.01
CUTOFF_SQ = 0.04
TIME_STEP = 0.05
CENTRE = 0.5

F32 = jnp.float32
BF16 = jnp.bfloat16
NT = (((1,), (1,)), ((), ()))
NN = (((1,), (0,)), ((), ()))
TN = (((0,), (0,)), ((), ()))
VMEM = pl.BlockSpec(memory_space=pltpu.VMEM)


def split3(value):
    high = value.astype(BF16).astype(F32)
    rest = value - high
    middle = rest.astype(BF16).astype(F32)
    return high, middle, rest - middle


def pair_parts(tile, row):
    xyz = jnp.where((row & 3) < 3, tile - CENTRE, 1.0)
    parts = split3(xyz)
    square = xyz * xyz
    norm = pltpu.roll(square, 1, 0) + pltpu.roll(square, 2, 0) + pltpu.roll(square, 3, 0)
    norms = split3(norm + jnp.where(row == 3, SOFTENING, 0.0))
    weights = split3(xyz * jnp.where(row < 4, tile[3:4], tile[7:8]))
    weights = jnp.concatenate([*weights, jnp.zeros_like(xyz)], axis=0).astype(BF16)
    return xyz, parts, norms, weights


def softened_distances(parts, norms, row):
    high, middle, low = parts
    minus_two = jnp.where(row < 3, -2.0, 0.0)
    one = jnp.where(row == 3, 1.0, 0.0)
    h2, m2, l2 = (pltpu.roll(part, 4, 0) * minus_two for part in parts)
    n0, n1, n2 = norms
    h3 = h2 + one
    lhs = [high, high, high] + [
        jnp.where(row == 3, norm, part) for norm, part in ((n0, middle), (n1, low), (n2, middle))
    ]
    rhs = [jnp.where(row == 7, norm, part) for norm, part in ((n0, h2), (n1, m2), (n2, l2))]
    rhs += [h3, h3, m2 + one]
    lhs = jnp.concatenate(lhs, axis=0).astype(BF16)
    rhs = jnp.concatenate(rhs, axis=0).astype(BF16)
    return lax.dot_general(lhs, rhs, TN, preferred_element_type=F32)


def pair_kernel(softened):
    taper = jnp.maximum((CUTOFF_SQ + SOFTENING) - softened, 0.0)
    root = lax.rsqrt(softened)
    scaled = taper * root
    kernel = scaled * scaled * root
    high = kernel.astype(BF16)
    return high, (kernel - high.astype(F32)).astype(BF16)


def moments(weights, kernel, half):
    high, low = kernel
    count = LEAF // 2 if half else LEAF
    twice = jnp.concatenate([weights, weights], axis=1)
    on_left = lax.dot_general(
        jnp.concatenate([high[:count], low[:count]], axis=1), twice, NT, preferred_element_type=F32
    ).T
    if half:
        on_left = jnp.concatenate([on_left, jnp.zeros_like(on_left)], axis=1)
    on_right = lax.dot_general(
        twice, jnp.concatenate([high, low], axis=0), NN, preferred_element_type=F32
    )
    return on_left, on_right


def force_tile(sums, xyz, row):
    on_left, on_right = (part[0:8] + part[8:16] + part[16:24] for part in sums)
    total = jnp.where(row < 4, on_right, on_left)
    mass = jnp.where(row < 4, total[3:4], total[7:8])
    return total - pltpu.roll(xyz, 4, 0) * mass


def pair_forces(tiles, row, half=False):
    count = len(tiles)
    parts, dists, sums, out = {}, {}, {}, []
    for step in range(count + 10):
        if step < count:
            parts[step] = pair_parts(tiles[step], row)
            dists[step] = softened_distances(parts[step][1], parts[step][2], row)
        k = step - 6
        if 0 <= k < count:
            sums[k] = moments(parts[k][3], pair_kernel(dists[k]), half)
        k = step - 10
        if k >= 0:
            out.append(force_tile(sums[k], parts[k][0], row))
    return out


def row_iota():
    return lax.broadcasted_iota(jnp.int32, (8, LEAF), 0)


def leaf_tile(state, leaf):
    return state[pl.ds(pl.multiple_of(leaf * 8, 8), 8), :]


def fill_slots(first, wanted, leaves, looked):
    parts = jnp.concatenate([part.astype(BF16) for part in split3(leaves)], axis=0)
    leaf = lax.broadcasted_iota(jnp.int32, (DEVICES, 3 * NLEAF), 1) & (NLEAF - 1)
    for turn in range(CAP):
        chosen = jnp.where(leaf == wanted[:, first + turn : first + turn + 1], 1.0, 0.0)
        found = lax.dot_general(chosen.astype(BF16), parts, NN, preferred_element_type=F32)
        for index in range(4):
            looked[pl.ds(4 * turn + index, DEVICES, stride=4 * CAP), :] = found[
                :, index * LEAF : (index + 1) * LEAF
            ]


def component(index):
    return slice(index * NLEAF, (index + 1) * NLEAF)


def store_state(state, index, value):
    state[pl.ds(index, NLEAF, stride=8), :] = value
    state[pl.ds(index + 4, NLEAF, stride=8), :] = value


def pack_kernel(
    positions, velocities, masses, bins, places0, places1,
    state, where, moving, placed0, placed1, order, ordered,
):
    placed0[...] = places0[...]
    placed1[...] = places1[...]
    for leaf in range(NLEAF):
        lanes = slice(leaf * LEAF, (leaf + 1) * LEAF)
        where[pl.ds(leaf, 3, stride=NLEAF), :] = positions[:, lanes]
        moving[pl.ds(leaf, 3, stride=NLEAF), :] = velocities[:, lanes]
    for index in range(3):
        store_state(state, index, where[component(index), :])
    store_state(state, 3, masses[...])
    kicked = jnp.where(bins[...] >= 3, 1.0, 0.0)
    earlier = lax.broadcasted_iota(jnp.int32, (LEAF, LEAF), 0) < lax.broadcasted_iota(
        jnp.int32, (LEAF, LEAF), 1
    )
    before = lax.dot_general(
        kicked.astype(BF16), jnp.where(earlier, 1.0, 0.0).astype(BF16), NN, preferred_element_type=F32
    )
    lane = lax.broadcasted_iota(jnp.int32, (NLEAF, LEAF), 1).astype(F32)
    last = jnp.sum(kicked, axis=1, keepdims=True) + lane - before
    order[...] = jnp.where(kicked > 0.0, before, last).astype(jnp.int32)

    def body(step, carry):
        for u in range(8):
            leaf = step * 8 + u
            moved = lax.dot_general(
                stacked(split3(leaf_tile(state, leaf))), lanes_of(order, leaf, LEAF), NT,
                preferred_element_type=F32,
            )
            ordered[pl.ds(pl.multiple_of(leaf * 8, 8), 8), :] = moved[0:8] + moved[8:16] + moved[16:24]
        return carry

    lax.fori_loop(0, NLEAF // 8, body, 0)


def stacked(parts):
    return jnp.concatenate([*parts, jnp.zeros_like(parts[0])], axis=0).astype(BF16)


def lanes_of(order, leaf, count):
    lane = lax.broadcasted_iota(jnp.int32, (count, LEAF), 0)
    return jnp.where(lane == order[pl.ds(leaf, 1), :], 1.0, 0.0).astype(BF16)


def gather_kernel(wanted, ordered, looked, asked, most):
    asked[...] = wanted[...].T[: 2 * CAP]
    most[...] = jnp.max(wanted[:, 2 * CAP : 2 * CAP + 1], axis=0, keepdims=True)
    leaves = [ordered[pl.ds(index, NLEAF, stride=8), :] for index in range(4)]
    fill_slots(0, wanted, jnp.concatenate(leaves, axis=1), looked)


def local_kernel(pairs, state, forces):
    row = row_iota()
    forces[...] = jnp.zeros_like(forces)
    unroll = 32

    def body(step, carry):
        ids = [
            (pairs[0, step * unroll + u], pairs[1, step * unroll + u])
            for u in range(unroll)
        ]
        found = pair_forces([jnp.where(row < 4, leaf_tile(state, a), leaf_tile(state, b)) for a, b in ids], row)
        for (a, b), force in zip(ids, found):
            to_left = pl.ds(pl.multiple_of(a * 8, 8), 8)
            to_right = pl.ds(pl.multiple_of(b * 8, 8), 8)
            forces[to_left, :] += jnp.where(row < 4, 0.0, force)
            forces[to_right, :] += jnp.where(row < 4, force, 0.0)
        return carry

    lax.fori_loop(0, LOCAL // unroll, body, 0)


def remote_kernel(unused, half, places, arrived, *refs):
    pushed, placed, sem, *apart = refs[unused:]
    forces = apart[0] if half else pushed
    row = row_iota()
    copy = pltpu.make_async_copy(places, placed, sem)
    copy.start()
    forces[...] = jnp.zeros_like(forces)
    copy.wait()
    unroll = 64

    def leaf(slot, side):
        tile = arrived[pl.ds(pl.multiple_of((slot >> 1) * 8, 8), 8), :]
        return jnp.where((slot & 1) == side, tile, pltpu.roll(tile, 4, 0))

    def body(step, carry):
        ids = [
            (placed[0, step * unroll + u], placed[1, step * unroll + u])
            for u in range(unroll)
        ]
        found = pair_forces([jnp.where(row < 4, leaf(a, 0), leaf(b, 1)) for a, b in ids], row, half)
        for (a, b), force in zip(ids, found):
            for slot, first in ((a, 4), (b, 0)):
                at = 3 * ((slot >> 1) + (slot & 1) * (SLOTS // 2)) if half else 3 * slot
                forces[pl.ds(at, 3), :] = force[first : first + 3]
        return carry

    lax.fori_loop(0, PAIRS // unroll, body, 0)
    if half:
        rows = pushed.shape[0]
        lower = lax.broadcasted_iota(jnp.int32, (rows, LEAF), 1) < LEAF // 2
        odd = pltpu.roll(forces[rows:, :], LEAF // 2, 1)
        pushed[...] = jnp.where(lower, forces[:rows, :], odd)


def summed(first, half, asked, returned):
    target = lax.broadcasted_iota(jnp.int32, (NLEAF, DEVICES), 0)
    chosen = [
        jnp.where(target == asked[first + turn : first + turn + 1, :], 1.0, 0.0) for turn in range(CAP)
    ]
    groups = CAP // 2 if half else CAP
    blocks = [
        jnp.concatenate(
            [returned[pl.ds(3 * group + index, DEVICES, stride=3 * groups), :] for index in range(3)],
            axis=1,
        )
        for group in range(groups)
    ]
    if half:
        even, odd = (jnp.concatenate(chosen[part::2], axis=1) for part in range(2))
        chosen = jnp.concatenate([even, odd], axis=0).astype(BF16)
    else:
        chosen = jnp.concatenate(chosen, axis=1).astype(BF16)
    total = jnp.zeros((chosen.shape[0], 3 * LEAF), F32)
    for part in split3(jnp.concatenate(blocks, axis=0)):
        total += lax.dot_general(chosen, part.astype(BF16), NN, preferred_element_type=F32)
    totals = [total[:, index * LEAF : (index + 1) * LEAF] for index in range(3)]
    if half:
        lower = lax.broadcasted_iota(jnp.int32, (NLEAF, LEAF), 1) < LEAF // 2
        totals = [
            jnp.where(lower, one[:NLEAF] + pltpu.roll(one[NLEAF:], LEAF // 2, 1), 0.0) for one in totals
        ]
    return totals


def disordered(totals, half, order, rows, spread):
    rows[:, 3 * NLEAF :, :] = jnp.zeros((3, 5 * NLEAF, LEAF), F32)
    for index, total in enumerate(totals):
        for number, part in enumerate(split3(total)):
            rows[number, component(index), :] = part
    count = LEAF // 2 if half else LEAF

    def body(step, carry):
        for u in range(64):
            leaf = step * 64 + u
            parts = [rows[number, pl.ds(leaf, 8, stride=NLEAF), :] for number in range(3)]
            moved = lax.dot_general(
                stacked(parts)[:, :count], lanes_of(order, leaf, count), NN, preferred_element_type=F32
            )
            moved = moved[0:8] + moved[8:16] + moved[16:24]
            spread[pl.ds(leaf, 3, stride=NLEAF), :] = moved[0:3]
        return carry

    lax.fori_loop(0, NLEAF // 64, body, 0)
    return [spread[component(index), :] for index in range(3)]


def kick_drift(threshold, totals, local, where, moving, bins):
    active = bins[...] >= threshold
    for index, accel in enumerate(totals):
        accel += local[pl.ds(index, NLEAF, stride=8), :] + local[pl.ds(index + 4, NLEAF, stride=8), :]
        accel *= 1.0 / CUTOFF_SQ**2
        velocity = moving[component(index), :] + jnp.where(active, TIME_STEP * accel, 0.0)
        yield index, accel, velocity, where[component(index), :] + TIME_STEP * velocity


def advance_kernel(
    half, wanted, asked, returned, local, masses, where, moving, bins, order,
    looked, state, new_where, new_moving, rows, spread,
):
    totals = disordered(summed(0, half, asked, returned), half, order, rows, spread)
    leaves = []
    for index, _, velocity, position in kick_drift(3, totals, local, where, moving, bins):
        new_moving[component(index), :] = velocity
        new_where[component(index), :] = position
        store_state(state, index, position)
        leaves.append(position)
    leaves.append(masses[...])
    fill_slots(CAP, wanted, jnp.concatenate(leaves, axis=1), looked)
    store_state(state, 3, masses[...])


def finish_kernel(asked, returned, local, where, moving, bins, positions, velocities, accels, rows):
    totals = summed(CAP, False, asked, returned)
    for index, *results in kick_drift(2, totals, local, where, moving, bins):
        for number, result in enumerate(results):
            rows[number, component(index), :] = result
    for leaf in range(NLEAF):
        lanes = slice(leaf * LEAF, (leaf + 1) * LEAF)
        for number, out in enumerate((accels, velocities, positions)):
            out[:, lanes] = rows[number, pl.ds(leaf, 3, stride=NLEAF), :]


def call(
    kernel, out_shapes, arrays, flops, size, scratch=(), in_specs=None, scalars=(), vmem=40 * 2**20
):
    return pl.pallas_call(
        kernel,
        out_shape=out_shapes,
        grid_spec=pltpu.PrefetchScalarGridSpec(
            num_scalar_prefetch=len(scalars),
            grid=(),
            in_specs=in_specs or [VMEM] * len(arrays),
            out_specs=jax.tree.map(lambda _: VMEM, out_shapes),
            scratch_shapes=scratch,
        ),
        compiler_params=pltpu.CompilerParams(vmem_limit_bytes=vmem),
        cost_estimate=pl.CostEstimate(flops=flops, bytes_accessed=size, transcendentals=0),
    )(*scalars, *arrays)


def shape(*dims, dtype=F32):
    return jax.ShapeDtypeStruct(dims, dtype)


def exchange(array):
    return lax.all_to_all(array, AXES, split_axis=0, concat_axis=0, tiled=True)


def send_leaves(looked):
    return exchange(looked.reshape(DEVICES, 4 * CAP, LEAF)).reshape(4 * SLOTS, LEAF)


def send_forces(pushed):
    return exchange(pushed.reshape(DEVICES, 3, -1, LEAF)).reshape(pushed.shape)


def request_kernel(pair_owner, pair_slot, time_bins, placed0, placed1, wanted, owners, slots, bins, sems):
    copies = [
        pltpu.make_async_copy(time_bins, bins, sems.at[2]),
        pltpu.make_async_copy(pair_owner, owners, sems.at[0]),
        pltpu.make_async_copy(pair_slot, slots, sems.at[1]),
    ]
    for copy in copies:
        copy.start()
    for copy in copies:
        copy.wait()
    ends = 2 * PAIRS
    owner_of = lax.broadcasted_iota(jnp.int32, (DEVICES, ends), 0)
    earlier = lax.broadcasted_iota(jnp.int32, (ends, ends), 0) < lax.broadcasted_iota(
        jnp.int32, (ends, ends), 1
    )
    earlier = jnp.where(earlier, 1.0, 0.0).astype(BF16)
    column = lax.broadcasted_iota(jnp.int32, (ends, LEAF), 1)
    total = jnp.zeros((DEVICES, LEAF), F32)
    for sub, placed in enumerate((placed0, placed1)):
        owner = jnp.concatenate([owners[sub, 0:1], owners[sub, 1:2]], axis=1)
        slot = jnp.concatenate([slots[sub, 0:1], slots[sub, 1:2]], axis=1) - NLEAF
        hit = jnp.where(owner_of == owner, 1.0, 0.0)
        before = lax.dot_general(hit.astype(BF16), earlier, NN, preferred_element_type=F32)
        rank = jnp.sum(hit * before, axis=0, keepdims=True)
        place = CAP * owner + rank.astype(jnp.int32)
        placed[0:1, :] = place[:, :PAIRS]
        placed[1:2, :] = place[:, PAIRS:]
        asked = hit * slot.astype(F32)
        for turn in range(CAP):
            mine = jnp.where(before == float(turn), asked, 0.0).astype(BF16)
            here = jnp.where(column == CAP * sub + turn, 1.0, 0.0).astype(BF16)
            total += lax.dot_general(mine, here, NN, preferred_element_type=F32)
    kicked = jnp.sum(jnp.where(bins[...] >= 3, 1.0, 0.0), axis=1, keepdims=True)
    most = jnp.max(kicked, axis=0, keepdims=True)
    lane = lax.broadcasted_iota(jnp.int32, (DEVICES, LEAF), 1)
    wanted[...] = jnp.where(lane == 2 * CAP, most, total + float(NLEAF)).astype(jnp.int32)


def shards(positions, velocities, masses, time_bins, pair_owner, pair_slot, local_pairs):
    masses = masses.reshape(NLEAF, LEAF)
    bins = time_bins.reshape(NLEAF, LEAF)
    local_ids = local_pairs.transpose(0, 2, 1)
    tiles_shape = shape(8 * NLEAF, LEAF)
    rows_shape = shape(3 * NLEAF, LEAF)
    looked_shape = shape(4 * SLOTS, LEAF)
    asked_shape = shape(2 * CAP, DEVICES, dtype=jnp.int32)
    ends_shape = shape(2, PAIRS, dtype=jnp.int32)
    anywhere = pl.BlockSpec(memory_space=pl.ANY)
    dma = pltpu.SemaphoreType.DMA

    def local_forces(ids, state):
        return call(local_kernel, tiles_shape, [state], 64 * 2**14 * 25, 2**20, scalars=[ids])

    def remote_forces(places, arrived, *earlier, half=False):
        scratch = [pltpu.SMEM((2, PAIRS), jnp.int32), dma(())]
        if half:
            scratch.append(pltpu.VMEM((3 * SLOTS, LEAF), F32))
        specs = [VMEM] * 2 + [anywhere] * len(earlier)
        return call(
            functools.partial(remote_kernel, len(earlier), half),
            shape((3 * SLOTS) // (2 if half else 1), LEAF),
            [places, arrived, *earlier],
            128 * 2**14 * 25,
            2**21,
            scratch,
            specs,
        )

    def subcycle0(half):
        def run(places, arrived, *arrays):
            returned = send_forces(remote_forces(places, arrived, half=half))
            wanted, asked, *others = arrays
            return call(
                functools.partial(advance_kernel, half),
                (looked_shape, tiles_shape, rows_shape, rows_shape),
                [wanted, asked, returned, *others],
                2**16,
                2**22,
                [pltpu.VMEM((3, 8 * NLEAF, LEAF), F32), pltpu.VMEM((3 * NLEAF, LEAF), F32)],
            )

        return run

    *placed, wanted = call(
        request_kernel,
        (ends_shape, ends_shape, shape(DEVICES, LEAF, dtype=jnp.int32)),
        [pair_owner.transpose(0, 2, 1), pair_slot.transpose(0, 2, 1), bins],
        2**26,
        2**18,
        [
            pltpu.VMEM((2, 2, PAIRS), jnp.int32),
            pltpu.VMEM((2, 2, PAIRS), jnp.int32),
            pltpu.VMEM((NLEAF, LEAF), jnp.int32),
            dma((3,)),
        ],
        [pl.BlockSpec(memory_space=pltpu.HBM)] * 3,
        vmem=60 * 2**20,
    )
    wanted = exchange(wanted.reshape(DEVICES, 1, LEAF)).reshape(DEVICES, LEAF)
    state, where, moving, *placed, order, ordered = call(
        pack_kernel,
        (
            tiles_shape, rows_shape, rows_shape, ends_shape, ends_shape,
            shape(NLEAF, LEAF, dtype=jnp.int32), tiles_shape,
        ),
        [positions, velocities, masses, bins, *placed],
        2**16,
        2**20,
    )
    looked, asked, most = call(
        gather_kernel,
        (looked_shape, shape(2 * CAP, DEVICES, dtype=jnp.int32), shape(1, 1, dtype=jnp.int32)),
        [wanted, ordered],
        2**16,
        2**21,
    )
    local = local_forces(local_ids[0], state)
    few = most[0, 0] <= LEAF // 2
    looked, state, where, moving = lax.cond(
        few, subcycle0(True), subcycle0(False),
        placed[0], send_leaves(looked), wanted, asked, local, masses, where, moving, bins, order,
    )
    local = local_forces(local_ids[1], state)
    pushed = remote_forces(placed[1], send_leaves(looked), local)
    returned = send_forces(pushed)
    out = shape(3, NLEAF * LEAF)
    return call(
        finish_kernel,
        (out, out, out),
        [asked, returned, local, where, moving, bins],
        2**16,
        2**22,
        [pltpu.VMEM((3, 3 * NLEAF, LEAF), F32)],
    )


def solution(mesh):
    split = P(None, AXES)
    rows = P(None, AXES, None)
    return jax.shard_map(
        shards,
        mesh=mesh,
        in_specs=(split, split, P(AXES), P(AXES), rows, rows, rows),
        out_specs=(split, split, split),
        check_vma=False,
    )
```

```python
import functools

import jax
import jax.numpy as jnp
from jax import lax
from jax.experimental import pallas as pl
from jax.experimental.pallas import tpu as pltpu
from jax.sharding import PartitionSpec as P

LEAF = 128
NLEAF = 64
DEVICES = 128
CAP = 4
PAIRS = 128
LOCAL = 64
SLOTS = DEVICES * CAP
AXES = ("gx", "gy", "gz")

SOFTENING = 0.01
CUTOFF_SQ = 0.04
TIME_STEP = 0.05
CENTRE = 0.5

F32 = jnp.float32
BF16 = jnp.bfloat16
NT = (((1,), (1,)), ((), ()))
NN = (((1,), (0,)), ((), ()))
TN = (((0,), (0,)), ((), ()))
VMEM = pl.BlockSpec(memory_space=pltpu.VMEM)


def split3(value):
    high = value.astype(BF16).astype(F32)
    rest = value - high
    middle = rest.astype(BF16).astype(F32)
    return high, middle, rest - middle


def pair_parts(tile, row):
    xyz = jnp.where((row & 3) < 3, tile - CENTRE, 1.0)
    parts = split3(xyz)
    square = xyz * xyz
    norm = pltpu.roll(square, 1, 0) + pltpu.roll(square, 2, 0) + pltpu.roll(square, 3, 0)
    norms = split3(norm + jnp.where(row == 3, SOFTENING, 0.0))
    weights = split3(xyz * jnp.where(row < 4, tile[3:4], tile[7:8]))
    weights = jnp.concatenate([*weights, jnp.zeros_like(xyz)], axis=0).astype(BF16)
    return xyz, parts, norms, weights


def softened_distances(parts, norms, row):
    high, middle, low = parts
    minus_two = jnp.where(row < 3, -2.0, 0.0)
    one = jnp.where(row == 3, 1.0, 0.0)
    h2, m2, l2 = (pltpu.roll(part, 4, 0) * minus_two for part in parts)
    n0, n1, n2 = norms
    h3 = h2 + one
    lhs = [high, high, high] + [
        jnp.where(row == 3, norm, part) for norm, part in ((n0, middle), (n1, low), (n2, middle))
    ]
    rhs = [jnp.where(row == 7, norm, part) for norm, part in ((n0, h2), (n1, m2), (n2, l2))]
    rhs += [h3, h3, m2 + one]
    lhs = jnp.concatenate(lhs, axis=0).astype(BF16)
    rhs = jnp.concatenate(rhs, axis=0).astype(BF16)
    return lax.dot_general(lhs, rhs, TN, preferred_element_type=F32)


def pair_kernel(softened):
    taper = jnp.maximum((CUTOFF_SQ + SOFTENING) - softened, 0.0)
    root = lax.rsqrt(softened)
    scaled = taper * root
    kernel = scaled * scaled * root
    high = kernel.astype(BF16)
    return high, (kernel - high.astype(F32)).astype(BF16)


def moments(weights, kernel, half):
    high, low = kernel
    count = LEAF // 2 if half else LEAF
    twice = jnp.concatenate([weights, weights], axis=1)
    on_left = lax.dot_general(
        jnp.concatenate([high[:count], low[:count]], axis=1), twice, NT, preferred_element_type=F32
    ).T
    if half:
        on_left = jnp.concatenate([on_left, jnp.zeros_like(on_left)], axis=1)
    on_right = lax.dot_general(
        twice, jnp.concatenate([high, low], axis=0), NN, preferred_element_type=F32
    )
    return on_left, on_right


def force_tile(sums, xyz, row):
    on_left, on_right = (part[0:8] + part[8:16] + part[16:24] for part in sums)
    total = jnp.where(row < 4, on_right, on_left)
    mass = jnp.where(row < 4, total[3:4], total[7:8])
    return total - pltpu.roll(xyz, 4, 0) * mass


def pair_forces(tiles, row, half=False):
    count = len(tiles)
    parts, dists, sums, out = {}, {}, {}, []
    for step in range(count + 10):
        if step < count:
            parts[step] = pair_parts(tiles[step], row)
            dists[step] = softened_distances(parts[step][1], parts[step][2], row)
        k = step - 6
        if 0 <= k < count:
            sums[k] = moments(parts[k][3], pair_kernel(dists[k]), half)
        k = step - 10
        if k >= 0:
            out.append(force_tile(sums[k], parts[k][0], row))
    return out


def row_iota():
    return lax.broadcasted_iota(jnp.int32, (8, LEAF), 0)


def leaf_tile(state, leaf):
    return state[pl.ds(pl.multiple_of(leaf * 8, 8), 8), :]


def fill_slots(first, wanted, leaves, looked):
    parts = jnp.concatenate([part.astype(BF16) for part in split3(leaves)], axis=0)
    leaf = lax.broadcasted_iota(jnp.int32, (DEVICES, 3 * NLEAF), 1) & (NLEAF - 1)
    for turn in range(CAP):
        chosen = jnp.where(leaf == wanted[:, first + turn : first + turn + 1], 1.0, 0.0)
        found = lax.dot_general(chosen.astype(BF16), parts, NN, preferred_element_type=F32)
        for index in range(4):
            looked[pl.ds(4 * turn + index, DEVICES, stride=4 * CAP), :] = found[
                :, index * LEAF : (index + 1) * LEAF
            ]


def component(index):
    return slice(index * NLEAF, (index + 1) * NLEAF)


def store_state(state, index, value):
    state[pl.ds(index, NLEAF, stride=8), :] = value
    state[pl.ds(index + 4, NLEAF, stride=8), :] = value


def pack_kernel(
    positions, velocities, masses, bins, places0, places1,
    state, where, moving, placed0, placed1, order, ordered, spread,
):
    placed0[...] = places0[...]
    placed1[...] = places1[...]
    for leaf in range(NLEAF):
        lanes = slice(leaf * LEAF, (leaf + 1) * LEAF)
        spread[0, pl.ds(leaf, 3, stride=NLEAF), :] = positions[:, lanes]
        spread[1, pl.ds(leaf, 3, stride=NLEAF), :] = velocities[:, lanes]
    where[...] = spread[0, : 3 * NLEAF, :]
    moving[...] = spread[1, : 3 * NLEAF, :]
    for index in range(3):
        store_state(state, index, where[component(index), :])
    store_state(state, 3, masses[...])
    kicked = jnp.where(bins[...] >= 3, 1.0, 0.0)
    earlier = lax.broadcasted_iota(jnp.int32, (LEAF, LEAF), 0) < lax.broadcasted_iota(
        jnp.int32, (LEAF, LEAF), 1
    )
    before = lax.dot_general(
        kicked.astype(BF16), jnp.where(earlier, 1.0, 0.0).astype(BF16), NN, preferred_element_type=F32
    )
    lane = lax.broadcasted_iota(jnp.int32, (NLEAF, LEAF), 1).astype(F32)
    last = jnp.sum(kicked, axis=1, keepdims=True) + lane - before
    order[...] = jnp.where(kicked > 0.0, before, last).astype(jnp.int32)

    for leaf in range(NLEAF):
        tile = slice(leaf * 8, leaf * 8 + 8)
        moved = lax.dot_general(
            stacked(split3(state[tile, :])), lanes_of(order, leaf, LEAF), NT, preferred_element_type=F32
        )
        ordered[tile, :] = moved[0:8] + moved[8:16] + moved[16:24]


def stacked(parts):
    return jnp.concatenate([*parts, jnp.zeros_like(parts[0])], axis=0).astype(BF16)


def lanes_of(order, leaf, count):
    lane = lax.broadcasted_iota(jnp.int32, (count, LEAF), 0)
    return jnp.where(lane == order[leaf : leaf + 1, :], 1.0, 0.0).astype(BF16)


def gather_kernel(wanted, ordered, looked, asked, most):
    asked[...] = wanted[...].T[: 2 * CAP]
    most[...] = jnp.max(wanted[:, 2 * CAP : 2 * CAP + 1], axis=0, keepdims=True)
    leaves = [ordered[pl.ds(index, NLEAF, stride=8), :] for index in range(4)]
    fill_slots(0, wanted, jnp.concatenate(leaves, axis=1), looked)


def local_kernel(pairs, state, forces):
    row = row_iota()
    forces[...] = jnp.zeros_like(forces)
    unroll = 32

    def body(step, carry):
        ids = [
            (pairs[0, step * unroll + u], pairs[1, step * unroll + u])
            for u in range(unroll)
        ]
        found = pair_forces([jnp.where(row < 4, leaf_tile(state, a), leaf_tile(state, b)) for a, b in ids], row)
        for (a, b), force in zip(ids, found):
            to_left = pl.ds(pl.multiple_of(a * 8, 8), 8)
            to_right = pl.ds(pl.multiple_of(b * 8, 8), 8)
            forces[to_left, :] += jnp.where(row < 4, 0.0, force)
            forces[to_right, :] += jnp.where(row < 4, force, 0.0)
        return carry

    lax.fori_loop(0, LOCAL // unroll, body, 0)


def remote_kernel(unused, half, places, arrived, *refs):
    pushed, placed, sem, forces = refs[unused:]
    row = row_iota()
    copy = pltpu.make_async_copy(places, placed, sem)
    copy.start()
    forces[...] = jnp.zeros_like(forces)
    copy.wait()
    unroll = 64

    def leaf(slot, side):
        tile = arrived[pl.ds(pl.multiple_of((slot >> 1) * 8, 8), 8), :]
        return jnp.where((slot & 1) == side, tile, pltpu.roll(tile, 4, 0))

    def body(step, carry):
        ids = [
            (placed[0, step * unroll + u], placed[1, step * unroll + u])
            for u in range(unroll)
        ]
        found = pair_forces([jnp.where(row < 4, leaf(a, 0), leaf(b, 1)) for a, b in ids], row, half)
        for (a, b), force in zip(ids, found):
            for slot, first in ((a, 4), (b, 0)):
                at = 3 * ((slot >> 1) + (slot & 1) * (SLOTS // 2)) if half else 3 * slot
                forces[pl.ds(at, 3), :] = force[first : first + 3]
        return carry

    lax.fori_loop(0, PAIRS // unroll, body, 0)
    if half:
        rows = pushed.shape[0]
        lower = lax.broadcasted_iota(jnp.int32, (rows, LEAF), 1) < LEAF // 2
        odd = pltpu.roll(forces[rows : 2 * rows, :], LEAF // 2, 1)
        pushed[...] = jnp.where(lower, forces[:rows, :], odd)
    else:
        pushed[...] = forces[: 3 * SLOTS, :]


def summed(first, half, asked, returned):
    target = lax.broadcasted_iota(jnp.int32, (NLEAF, DEVICES), 0)
    chosen = [
        jnp.where(target == asked[first + turn : first + turn + 1, :], 1.0, 0.0) for turn in range(CAP)
    ]
    groups = CAP // 2 if half else CAP
    blocks = [
        jnp.concatenate(
            [returned[pl.ds(3 * group + index, DEVICES, stride=3 * groups), :] for index in range(3)],
            axis=1,
        )
        for group in range(groups)
    ]
    if half:
        even, odd = (jnp.concatenate(chosen[part::2], axis=1) for part in range(2))
        chosen = jnp.concatenate([even, odd], axis=0).astype(BF16)
    else:
        chosen = jnp.concatenate(chosen, axis=1).astype(BF16)
    total = jnp.zeros((chosen.shape[0], 3 * LEAF), F32)
    for part in split3(jnp.concatenate(blocks, axis=0)):
        total += lax.dot_general(chosen, part.astype(BF16), NN, preferred_element_type=F32)
    totals = [total[:, index * LEAF : (index + 1) * LEAF] for index in range(3)]
    if half:
        lower = lax.broadcasted_iota(jnp.int32, (NLEAF, LEAF), 1) < LEAF // 2
        totals = [
            jnp.where(lower, one[:NLEAF] + pltpu.roll(one[NLEAF:], LEAF // 2, 1), 0.0) for one in totals
        ]
    return totals


def disordered(totals, half, order, rows, spread):
    rows[:, 3 * NLEAF :, :] = jnp.zeros((3, 5 * NLEAF, LEAF), F32)
    for index, total in enumerate(totals):
        for number, part in enumerate(split3(total)):
            rows[number, component(index), :] = part
    count = LEAF // 2 if half else LEAF

    for leaf in range(NLEAF):
        parts = [rows[number, pl.ds(leaf, 8, stride=NLEAF), :] for number in range(3)]
        moved = lax.dot_general(
            stacked(parts)[:, :count], lanes_of(order, leaf, count), NN, preferred_element_type=F32
        )
        spread[pl.ds(leaf, 8, stride=NLEAF), :] = moved[0:8] + moved[8:16] + moved[16:24]
    return [spread[component(index), :] for index in range(3)]


def kick_drift(threshold, totals, local, where, moving, bins):
    active = bins[...] >= threshold
    for index, accel in enumerate(totals):
        accel += local[pl.ds(index, NLEAF, stride=8), :] + local[pl.ds(index + 4, NLEAF, stride=8), :]
        accel *= 1.0 / CUTOFF_SQ**2
        velocity = moving[component(index), :] + jnp.where(active, TIME_STEP * accel, 0.0)
        yield index, accel, velocity, where[component(index), :] + TIME_STEP * velocity


def advance_kernel(
    half, wanted, asked, returned, local, masses, where, moving, bins, order,
    looked, state, new_where, new_moving, rows, spread,
):
    totals = disordered(summed(0, half, asked, returned), half, order, rows, spread)
    leaves = []
    for index, _, velocity, position in kick_drift(3, totals, local, where, moving, bins):
        new_moving[component(index), :] = velocity
        new_where[component(index), :] = position
        store_state(state, index, position)
        leaves.append(position)
    leaves.append(masses[...])
    fill_slots(CAP, wanted, jnp.concatenate(leaves, axis=1), looked)
    store_state(state, 3, masses[...])


def finish_kernel(asked, returned, local, where, moving, bins, positions, velocities, accels, rows):
    totals = summed(CAP, False, asked, returned)
    for index, *results in kick_drift(2, totals, local, where, moving, bins):
        for number, result in enumerate(results):
            rows[number, component(index), :] = result
    for leaf in range(NLEAF):
        lanes = slice(leaf * LEAF, (leaf + 1) * LEAF)
        for number, out in enumerate((accels, velocities, positions)):
            out[:, lanes] = rows[number, pl.ds(leaf, 3, stride=NLEAF), :]


def call(
    kernel, out_shapes, arrays, flops, size, scratch=(), in_specs=None, scalars=(), vmem=40 * 2**20
):
    return pl.pallas_call(
        kernel,
        out_shape=out_shapes,
        grid_spec=pltpu.PrefetchScalarGridSpec(
            num_scalar_prefetch=len(scalars),
            grid=(),
            in_specs=in_specs or [VMEM] * len(arrays),
            out_specs=jax.tree.map(lambda _: VMEM, out_shapes),
            scratch_shapes=scratch,
        ),
        compiler_params=pltpu.CompilerParams(vmem_limit_bytes=vmem),
        cost_estimate=pl.CostEstimate(flops=flops, bytes_accessed=size, transcendentals=0),
    )(*scalars, *arrays)


def shape(*dims, dtype=F32):
    return jax.ShapeDtypeStruct(dims, dtype)


def exchange(array):
    return lax.all_to_all(array, AXES, split_axis=0, concat_axis=0, tiled=True)


def send_leaves(looked):
    return exchange(looked.reshape(DEVICES, 4 * CAP, LEAF)).reshape(4 * SLOTS, LEAF)


def send_forces(pushed):
    return exchange(pushed.reshape(DEVICES, 3, -1, LEAF)).reshape(pushed.shape)


def request_kernel(pair_owner, pair_slot, time_bins, placed0, placed1, wanted, owners, slots, bins, sems):
    copies = [
        pltpu.make_async_copy(time_bins, bins, sems.at[2]),
        pltpu.make_async_copy(pair_owner, owners, sems.at[0]),
        pltpu.make_async_copy(pair_slot, slots, sems.at[1]),
    ]
    for copy in copies:
        copy.start()
    for copy in copies:
        copy.wait()
    ends = 2 * PAIRS
    owner_of = lax.broadcasted_iota(jnp.int32, (DEVICES, ends), 0)
    earlier = lax.broadcasted_iota(jnp.int32, (ends, ends), 0) < lax.broadcasted_iota(
        jnp.int32, (ends, ends), 1
    )
    earlier = jnp.where(earlier, 1.0, 0.0).astype(BF16)
    column = lax.broadcasted_iota(jnp.int32, (ends, LEAF), 1)
    total = jnp.zeros((DEVICES, LEAF), F32)
    for sub, placed in enumerate((placed0, placed1)):
        owner = jnp.concatenate([owners[sub, 0:1], owners[sub, 1:2]], axis=1)
        slot = jnp.concatenate([slots[sub, 0:1], slots[sub, 1:2]], axis=1) - NLEAF
        hit = jnp.where(owner_of == owner, 1.0, 0.0)
        before = lax.dot_general(hit.astype(BF16), earlier, NN, preferred_element_type=F32)
        rank = jnp.sum(hit * before, axis=0, keepdims=True)
        place = CAP * owner + rank.astype(jnp.int32)
        placed[0:1, :] = place[:, :PAIRS]
        placed[1:2, :] = place[:, PAIRS:]
        asked = hit * slot.astype(F32)
        for turn in range(CAP):
            mine = jnp.where(before == float(turn), asked, 0.0).astype(BF16)
            here = jnp.where(column == CAP * sub + turn, 1.0, 0.0).astype(BF16)
            total += lax.dot_general(mine, here, NN, preferred_element_type=F32)
    kicked = jnp.sum(jnp.where(bins[...] >= 3, 1.0, 0.0), axis=1, keepdims=True)
    most = jnp.max(kicked, axis=0, keepdims=True)
    lane = lax.broadcasted_iota(jnp.int32, (DEVICES, LEAF), 1)
    wanted[...] = jnp.where(lane == 2 * CAP, most, total + float(NLEAF)).astype(jnp.int32)


def shards(positions, velocities, masses, time_bins, pair_owner, pair_slot, local_pairs):
    masses = masses.reshape(NLEAF, LEAF)
    bins = time_bins.reshape(NLEAF, LEAF)
    local_ids = local_pairs.transpose(0, 2, 1)
    tiles_shape = shape(8 * NLEAF, LEAF)
    rows_shape = shape(3 * NLEAF, LEAF)
    looked_shape = shape(4 * SLOTS, LEAF)
    asked_shape = shape(2 * CAP, DEVICES, dtype=jnp.int32)
    ends_shape = shape(2, PAIRS, dtype=jnp.int32)
    anywhere = pl.BlockSpec(memory_space=pl.ANY)
    dma = pltpu.SemaphoreType.DMA

    def local_forces(ids, state):
        return call(local_kernel, tiles_shape, [state], 64 * 2**14 * 25, 2**20, scalars=[ids])

    def remote_forces(places, arrived, *earlier, half=False):
        scratch = [pltpu.SMEM((2, PAIRS), jnp.int32), dma(())]
        scratch.append(pltpu.VMEM((3 * SLOTS + 8, LEAF), F32))
        specs = [VMEM] * 2 + [anywhere] * len(earlier)
        return call(
            functools.partial(remote_kernel, len(earlier), half),
            shape((3 * SLOTS) // (2 if half else 1), LEAF),
            [places, arrived, *earlier],
            128 * 2**14 * 25,
            2**21,
            scratch,
            specs,
        )

    def subcycle0(half):
        def run(places, arrived, *arrays):
            returned = send_forces(remote_forces(places, arrived, half=half))
            wanted, asked, *others = arrays
            return call(
                functools.partial(advance_kernel, half),
                (looked_shape, tiles_shape, rows_shape, rows_shape),
                [wanted, asked, returned, *others],
                2**16,
                2**22,
                [pltpu.VMEM((3, 8 * NLEAF, LEAF), F32), pltpu.VMEM((8 * NLEAF, LEAF), F32)],
            )

        return run

    *placed, wanted = call(
        request_kernel,
        (ends_shape, ends_shape, shape(DEVICES, LEAF, dtype=jnp.int32)),
        [pair_owner.transpose(0, 2, 1), pair_slot.transpose(0, 2, 1), bins],
        2**26,
        2**18,
        [
            pltpu.VMEM((2, 2, PAIRS), jnp.int32),
            pltpu.VMEM((2, 2, PAIRS), jnp.int32),
            pltpu.VMEM((NLEAF, LEAF), jnp.int32),
            dma((3,)),
        ],
        [pl.BlockSpec(memory_space=pltpu.HBM)] * 3,
        vmem=60 * 2**20,
    )
    wanted = exchange(wanted.reshape(DEVICES, 1, LEAF)).reshape(DEVICES, LEAF)
    state, where, moving, *placed, order, ordered = call(
        pack_kernel,
        (
            tiles_shape, rows_shape, rows_shape, ends_shape, ends_shape,
            shape(NLEAF, LEAF, dtype=jnp.int32), tiles_shape,
        ),
        [positions, velocities, masses, bins, *placed],
        2**16,
        2**20,
        [pltpu.VMEM((2, 8 * NLEAF, LEAF), F32)],
    )
    looked, asked, most = call(
        gather_kernel,
        (looked_shape, shape(2 * CAP, DEVICES, dtype=jnp.int32), shape(1, 1, dtype=jnp.int32)),
        [wanted, ordered],
        2**16,
        2**21,
    )
    local = local_forces(local_ids[0], state)
    few = most[0, 0] <= LEAF // 2
    looked, state, where, moving = lax.cond(
        few, subcycle0(True), subcycle0(False),
        placed[0], send_leaves(looked), wanted, asked, local, masses, where, moving, bins, order,
    )
    local = local_forces(local_ids[1], state)
    pushed = remote_forces(placed[1], send_leaves(looked), local)
    returned = send_forces(pushed)
    out = shape(3, NLEAF * LEAF)
    return call(
        finish_kernel,
        (out, out, out),
        [asked, returned, local, where, moving, bins],
        2**16,
        2**22,
        [pltpu.VMEM((3, 8 * NLEAF, LEAF), F32)],
    )


def solution(mesh):
    split = P(None, AXES)
    rows = P(None, AXES, None)
    return jax.shard_map(
        shards,
        mesh=mesh,
        in_specs=(split, split, P(AXES), P(AXES), rows, rows, rows),
        out_specs=(split, split, split),
        check_vma=False,
    )
```

```python
import functools

import jax
import jax.numpy as jnp
from jax import lax
from jax.experimental import pallas as pl
from jax.experimental.pallas import tpu as pltpu
from jax.sharding import PartitionSpec as P

LEAF = 128
NLEAF = 64
DEVICES = 128
CAP = 4
PAIRS = 128
LOCAL = 64
SLOTS = DEVICES * CAP
AXES = ("gx", "gy", "gz")

SOFTENING = 0.01
CUTOFF_SQ = 0.04
TIME_STEP = 0.05
CENTRE = 0.5

F32 = jnp.float32
BF16 = jnp.bfloat16
NT = (((1,), (1,)), ((), ()))
NN = (((1,), (0,)), ((), ()))
TN = (((0,), (0,)), ((), ()))
VMEM = pl.BlockSpec(memory_space=pltpu.VMEM)


def split3(value):
    high = value.astype(BF16).astype(F32)
    rest = value - high
    middle = rest.astype(BF16).astype(F32)
    return high, middle, rest - middle


def pair_parts(tile, row):
    xyz = jnp.where((row & 3) < 3, tile - CENTRE, 1.0)
    parts = split3(xyz)
    square = xyz * xyz
    norm = pltpu.roll(square, 1, 0) + pltpu.roll(square, 2, 0) + pltpu.roll(square, 3, 0)
    norms = split3(norm + jnp.where(row == 3, SOFTENING, 0.0))
    weights = split3(xyz * jnp.where(row < 4, tile[3:4], tile[7:8]))
    weights = jnp.concatenate([*weights, jnp.zeros_like(xyz)], axis=0).astype(BF16)
    return xyz, parts, norms, weights


def softened_distances(parts, norms, row):
    high, middle, low = parts
    minus_two = jnp.where(row < 3, -2.0, 0.0)
    one = jnp.where(row == 3, 1.0, 0.0)
    h2, m2, l2 = (pltpu.roll(part, 4, 0) * minus_two for part in parts)
    n0, n1, n2 = norms
    h3 = h2 + one
    lhs = [high, high, high] + [
        jnp.where(row == 3, norm, part) for norm, part in ((n0, middle), (n1, low), (n2, middle))
    ]
    rhs = [jnp.where(row == 7, norm, part) for norm, part in ((n0, h2), (n1, m2), (n2, l2))]
    rhs += [h3, h3, m2 + one]
    lhs = jnp.concatenate(lhs, axis=0).astype(BF16)
    rhs = jnp.concatenate(rhs, axis=0).astype(BF16)
    return lax.dot_general(lhs, rhs, TN, preferred_element_type=F32)


def pair_kernel(softened):
    taper = jnp.maximum((CUTOFF_SQ + SOFTENING) - softened, 0.0)
    root = lax.rsqrt(softened)
    scaled = taper * root
    kernel = scaled * scaled * root
    high = kernel.astype(BF16)
    return high, (kernel - high.astype(F32)).astype(BF16)


def moments(weights, kernel, half):
    high, low = kernel
    count = LEAF // 2 if half else LEAF
    twice = jnp.concatenate([weights, weights], axis=1)
    on_left = lax.dot_general(
        jnp.concatenate([high[:count], low[:count]], axis=1), twice, NT, preferred_element_type=F32
    ).T
    if half:
        on_left = jnp.concatenate([on_left, jnp.zeros_like(on_left)], axis=1)
    on_right = lax.dot_general(
        twice, jnp.concatenate([high, low], axis=0), NN, preferred_element_type=F32
    )
    return on_left, on_right


def force_tile(sums, xyz, row):
    on_left, on_right = (part[0:8] + part[8:16] + part[16:24] for part in sums)
    total = jnp.where(row < 4, on_right, on_left)
    mass = jnp.where(row < 4, total[3:4], total[7:8])
    return total - pltpu.roll(xyz, 4, 0) * mass


def pair_forces(tiles, row, half=False):
    count = len(tiles)
    parts, dists, sums, out = {}, {}, {}, []
    for step in range(count + 10):
        if step < count:
            parts[step] = pair_parts(tiles[step], row)
            dists[step] = softened_distances(parts[step][1], parts[step][2], row)
        k = step - 6
        if 0 <= k < count:
            sums[k] = moments(parts[k][3], pair_kernel(dists[k]), half)
        k = step - 10
        if k >= 0:
            out.append(force_tile(sums[k], parts[k][0], row))
    return out


def row_iota():
    return lax.broadcasted_iota(jnp.int32, (8, LEAF), 0)


def leaf_tile(state, leaf):
    return state[pl.ds(pl.multiple_of(leaf * 8, 8), 8), :]


def fill_slots(first, wanted, leaves, looked):
    parts = jnp.concatenate([part.astype(BF16) for part in split3(leaves)], axis=0)
    leaf = lax.broadcasted_iota(jnp.int32, (DEVICES, 3 * NLEAF), 1) & (NLEAF - 1)
    for turn in range(CAP):
        chosen = jnp.where(leaf == wanted[:, first + turn : first + turn + 1], 1.0, 0.0)
        found = lax.dot_general(chosen.astype(BF16), parts, NN, preferred_element_type=F32)
        for index in range(4):
            looked[pl.ds(4 * turn + index, DEVICES, stride=4 * CAP), :] = found[
                :, index * LEAF : (index + 1) * LEAF
            ]


def component(index):
    return slice(index * NLEAF, (index + 1) * NLEAF)


def store_state(state, index, value):
    state[pl.ds(index, NLEAF, stride=8), :] = value
    state[pl.ds(index + 4, NLEAF, stride=8), :] = value


def pack_kernel(
    positions, velocities, masses, bins, places0, places1,
    state, where, moving, placed0, placed1, order, ordered, spread,
):
    placed0[...] = places0[...]
    placed1[...] = places1[...]
    for leaf in range(NLEAF):
        lanes = slice(leaf * LEAF, (leaf + 1) * LEAF)
        spread[0, pl.ds(leaf, 3, stride=NLEAF), :] = positions[:, lanes]
        spread[1, pl.ds(leaf, 3, stride=NLEAF), :] = velocities[:, lanes]
    where[...] = spread[0, : 3 * NLEAF, :]
    moving[...] = spread[1, : 3 * NLEAF, :]
    for index in range(3):
        store_state(state, index, where[component(index), :])
    store_state(state, 3, masses[...])
    kicked = jnp.where(bins[...] >= 3, 1.0, 0.0)
    earlier = lax.broadcasted_iota(jnp.int32, (LEAF, LEAF), 0) < lax.broadcasted_iota(
        jnp.int32, (LEAF, LEAF), 1
    )
    before = lax.dot_general(
        kicked.astype(BF16), jnp.where(earlier, 1.0, 0.0).astype(BF16), NN, preferred_element_type=F32
    )
    lane = lax.broadcasted_iota(jnp.int32, (NLEAF, LEAF), 1).astype(F32)
    last = jnp.sum(kicked, axis=1, keepdims=True) + lane - before
    order[...] = jnp.where(kicked > 0.0, before, last).astype(jnp.int32)

    for leaf in range(NLEAF):
        tile = slice(leaf * 8, leaf * 8 + 8)
        moved = lax.dot_general(
            stacked(split3(state[tile, :])), lanes_of(order, leaf, LEAF), NT, preferred_element_type=F32
        )
        ordered[tile, :] = moved[0:8] + moved[8:16] + moved[16:24]


def stacked(parts):
    return jnp.concatenate([*parts, jnp.zeros_like(parts[0])], axis=0).astype(BF16)


def lanes_of(order, leaf, count):
    lane = lax.broadcasted_iota(jnp.int32, (count, LEAF), 0)
    return jnp.where(lane == order[leaf : leaf + 1, :], 1.0, 0.0).astype(BF16)


def gather_kernel(wanted, ordered, looked, asked, most):
    asked[...] = wanted[...].T[: 2 * CAP]
    most[...] = jnp.max(wanted[:, 2 * CAP : 2 * CAP + 1], axis=0, keepdims=True)
    leaves = [ordered[pl.ds(index, NLEAF, stride=8), :] for index in range(4)]
    fill_slots(0, wanted, jnp.concatenate(leaves, axis=1), looked)


def local_kernel(pairs, state, forces):
    row = row_iota()
    forces[...] = jnp.zeros_like(forces)
    unroll = 32

    def body(step, carry):
        ids = [
            (pairs[0, step * unroll + u], pairs[1, step * unroll + u])
            for u in range(unroll)
        ]
        found = pair_forces([jnp.where(row < 4, leaf_tile(state, a), leaf_tile(state, b)) for a, b in ids], row)
        for (a, b), force in zip(ids, found):
            to_left = pl.ds(pl.multiple_of(a * 8, 8), 8)
            to_right = pl.ds(pl.multiple_of(b * 8, 8), 8)
            forces[to_left, :] += jnp.where(row < 4, 0.0, force)
            forces[to_right, :] += jnp.where(row < 4, force, 0.0)
        return carry

    lax.fori_loop(0, LOCAL // unroll, body, 0)


def remote_kernel(unused, half, places, arrived, *refs):
    pushed, placed, sem, forces = refs[unused:]
    row = row_iota()
    copy = pltpu.make_async_copy(places, placed, sem)
    copy.start()
    forces[...] = jnp.zeros_like(forces)
    copy.wait()
    unroll = 64

    def leaf(slot, side):
        tile = arrived[pl.ds(pl.multiple_of((slot >> 1) * 8, 8), 8), :]
        return jnp.where((slot & 1) == side, tile, pltpu.roll(tile, 4, 0))

    def body(step, carry):
        ids = [
            (placed[0, step * unroll + u], placed[1, step * unroll + u])
            for u in range(unroll)
        ]
        found = pair_forces([jnp.where(row < 4, leaf(a, 0), leaf(b, 1)) for a, b in ids], row, half)
        for (a, b), force in zip(ids, found):
            for slot, first in ((a, 4), (b, 0)):
                at = 3 * ((slot >> 1) + (slot & 1) * (SLOTS // 2)) if half else 3 * slot
                forces[pl.ds(at, 3), :] = force[first : first + 3]
        return carry

    lax.fori_loop(0, PAIRS // unroll, body, 0)
    if half:
        rows = pushed.shape[0]
        lower = lax.broadcasted_iota(jnp.int32, (rows, LEAF), 1) < LEAF // 2
        odd = pltpu.roll(forces[rows : 2 * rows, :], LEAF // 2, 1)
        pushed[...] = jnp.where(lower, forces[:rows, :], odd)
    else:
        pushed[...] = forces[: 3 * SLOTS, :]


def summed(first, half, asked, returned):
    target = lax.broadcasted_iota(jnp.int32, (NLEAF, DEVICES), 0)
    chosen = [
        jnp.where(target == asked[first + turn : first + turn + 1, :], 1.0, 0.0) for turn in range(CAP)
    ]
    groups = CAP // 2 if half else CAP
    blocks = [
        jnp.concatenate(
            [returned[pl.ds(3 * group + index, DEVICES, stride=3 * groups), :] for index in range(3)],
            axis=1,
        )
        for group in range(groups)
    ]
    if half:
        even, odd = (jnp.concatenate(chosen[part::2], axis=1) for part in range(2))
        chosen = jnp.concatenate([even, odd], axis=0).astype(BF16)
    else:
        chosen = jnp.concatenate(chosen, axis=1).astype(BF16)
    total = jnp.zeros((chosen.shape[0], 3 * LEAF), F32)
    for part in split3(jnp.concatenate(blocks, axis=0)):
        total += lax.dot_general(chosen, part.astype(BF16), NN, preferred_element_type=F32)
    totals = [total[:, index * LEAF : (index + 1) * LEAF] for index in range(3)]
    if half:
        lower = lax.broadcasted_iota(jnp.int32, (NLEAF, LEAF), 1) < LEAF // 2
        totals = [
            jnp.where(lower, one[:NLEAF] + pltpu.roll(one[NLEAF:], LEAF // 2, 1), 0.0) for one in totals
        ]
    return totals


def disordered(totals, half, order, rows, spread):
    rows[:, 3 * NLEAF :, :] = jnp.zeros((3, 5 * NLEAF, LEAF), F32)
    for index, total in enumerate(totals):
        for number, part in enumerate(split3(total)):
            rows[number, component(index), :] = part
    count = LEAF // 2 if half else LEAF

    for leaf in range(NLEAF):
        parts = [rows[number, pl.ds(leaf, 8, stride=NLEAF), :] for number in range(3)]
        moved = lax.dot_general(
            stacked(parts)[:, :count], lanes_of(order, leaf, count), NN, preferred_element_type=F32
        )
        spread[pl.ds(leaf, 8, stride=NLEAF), :] = moved[0:8] + moved[8:16] + moved[16:24]
    return [spread[component(index), :] for index in range(3)]


def kick_drift(threshold, totals, local, where, moving, bins):
    active = bins[...] >= threshold
    for index, accel in enumerate(totals):
        accel += local[pl.ds(index, NLEAF, stride=8), :] + local[pl.ds(index + 4, NLEAF, stride=8), :]
        accel *= 1.0 / CUTOFF_SQ**2
        velocity = moving[component(index), :] + jnp.where(active, TIME_STEP * accel, 0.0)
        yield index, accel, velocity, where[component(index), :] + TIME_STEP * velocity


def advance_kernel(
    half, wanted, asked, returned, local, masses, where, moving, bins, order,
    looked, state, new_where, new_moving, rows, spread,
):
    totals = disordered(summed(0, half, asked, returned), half, order, rows, spread)
    leaves = []
    for index, _, velocity, position in kick_drift(3, totals, local, where, moving, bins):
        new_moving[component(index), :] = velocity
        new_where[component(index), :] = position
        store_state(state, index, position)
        leaves.append(position)
    leaves.append(masses[...])
    fill_slots(CAP, wanted, jnp.concatenate(leaves, axis=1), looked)
    store_state(state, 3, masses[...])


def finish_kernel(
    asked, returned, local, where, moving, bins, positions, velocities, accels, rows, *scratch
):
    staged, sems = scratch[:3], scratch[3]
    totals = summed(CAP, False, asked, returned)
    for index, *results in kick_drift(2, totals, local, where, moving, bins):
        for number, result in enumerate(results):
            rows[number, component(index), :] = result
    copies = []
    for number, out in enumerate((accels, velocities, positions)):
        for leaf in range(NLEAF):
            lanes = slice(leaf * LEAF, (leaf + 1) * LEAF)
            staged[number][:, lanes] = rows[number, pl.ds(leaf, 3, stride=NLEAF), :]
        copies.append(pltpu.make_async_copy(staged[number], out, sems.at[number]))
        copies[-1].start()
    for copy in copies:
        copy.wait()


def call(
    kernel, out_shapes, arrays, flops, size, scratch=(), in_specs=None, scalars=(), vmem=40 * 2**20,
    out_specs=None,
):
    return pl.pallas_call(
        kernel,
        out_shape=out_shapes,
        grid_spec=pltpu.PrefetchScalarGridSpec(
            num_scalar_prefetch=len(scalars),
            grid=(),
            in_specs=in_specs or [VMEM] * len(arrays),
            out_specs=out_specs or jax.tree.map(lambda _: VMEM, out_shapes),
            scratch_shapes=scratch,
        ),
        compiler_params=pltpu.CompilerParams(vmem_limit_bytes=vmem),
        cost_estimate=pl.CostEstimate(flops=flops, bytes_accessed=size, transcendentals=0),
    )(*scalars, *arrays)


def shape(*dims, dtype=F32):
    return jax.ShapeDtypeStruct(dims, dtype)


def exchange(array):
    return lax.all_to_all(array, AXES, split_axis=0, concat_axis=0, tiled=True)


def send_leaves(looked):
    return exchange(looked.reshape(DEVICES, 4 * CAP, LEAF)).reshape(4 * SLOTS, LEAF)


def send_forces(pushed):
    return exchange(pushed.reshape(DEVICES, 3, -1, LEAF)).reshape(pushed.shape)


def request_kernel(pair_owner, pair_slot, time_bins, placed0, placed1, wanted, owners, slots, bins, sems):
    copies = [
        pltpu.make_async_copy(time_bins, bins, sems.at[2]),
        pltpu.make_async_copy(pair_owner, owners, sems.at[0]),
        pltpu.make_async_copy(pair_slot, slots, sems.at[1]),
    ]
    for copy in copies:
        copy.start()
    for copy in copies:
        copy.wait()
    ends = 2 * PAIRS
    owner_of = lax.broadcasted_iota(jnp.int32, (DEVICES, ends), 0)
    earlier = lax.broadcasted_iota(jnp.int32, (ends, ends), 0) < lax.broadcasted_iota(
        jnp.int32, (ends, ends), 1
    )
    earlier = jnp.where(earlier, 1.0, 0.0).astype(BF16)
    column = lax.broadcasted_iota(jnp.int32, (ends, LEAF), 1)
    total = jnp.zeros((DEVICES, LEAF), F32)
    for sub, placed in enumerate((placed0, placed1)):
        owner = jnp.concatenate([owners[sub, 0:1], owners[sub, 1:2]], axis=1)
        slot = jnp.concatenate([slots[sub, 0:1], slots[sub, 1:2]], axis=1) - NLEAF
        hit = jnp.where(owner_of == owner, 1.0, 0.0)
        before = lax.dot_general(hit.astype(BF16), earlier, NN, preferred_element_type=F32)
        rank = jnp.sum(hit * before, axis=0, keepdims=True)
        place = CAP * owner + rank.astype(jnp.int32)
        placed[0:1, :] = place[:, :PAIRS]
        placed[1:2, :] = place[:, PAIRS:]
        asked = hit * slot.astype(F32)
        for turn in range(CAP):
            mine = jnp.where(before == float(turn), asked, 0.0).astype(BF16)
            here = jnp.where(column == CAP * sub + turn, 1.0, 0.0).astype(BF16)
            total += lax.dot_general(mine, here, NN, preferred_element_type=F32)
    kicked = jnp.sum(jnp.where(bins[...] >= 3, 1.0, 0.0), axis=1, keepdims=True)
    most = jnp.max(kicked, axis=0, keepdims=True)
    lane = lax.broadcasted_iota(jnp.int32, (DEVICES, LEAF), 1)
    wanted[...] = jnp.where(lane == 2 * CAP, most, total + float(NLEAF)).astype(jnp.int32)


def shards(positions, velocities, masses, time_bins, pair_owner, pair_slot, local_pairs):
    masses = masses.reshape(NLEAF, LEAF)
    bins = time_bins.reshape(NLEAF, LEAF)
    local_ids = local_pairs.transpose(0, 2, 1)
    tiles_shape = shape(8 * NLEAF, LEAF)
    rows_shape = shape(3 * NLEAF, LEAF)
    looked_shape = shape(4 * SLOTS, LEAF)
    asked_shape = shape(2 * CAP, DEVICES, dtype=jnp.int32)
    ends_shape = shape(2, PAIRS, dtype=jnp.int32)
    anywhere = pl.BlockSpec(memory_space=pl.ANY)
    dma = pltpu.SemaphoreType.DMA

    def local_forces(ids, state):
        return call(local_kernel, tiles_shape, [state], 64 * 2**14 * 25, 2**20, scalars=[ids])

    def remote_forces(places, arrived, *earlier, half=False):
        scratch = [pltpu.SMEM((2, PAIRS), jnp.int32), dma(())]
        scratch.append(pltpu.VMEM((3 * SLOTS + 8, LEAF), F32))
        specs = [VMEM] * 2 + [anywhere] * len(earlier)
        return call(
            functools.partial(remote_kernel, len(earlier), half),
            shape((3 * SLOTS) // (2 if half else 1), LEAF),
            [places, arrived, *earlier],
            128 * 2**14 * 25,
            2**21,
            scratch,
            specs,
        )

    def subcycle0(half):
        def run(places, arrived, *arrays):
            returned = send_forces(remote_forces(places, arrived, half=half))
            wanted, asked, *others = arrays
            return call(
                functools.partial(advance_kernel, half),
                (looked_shape, tiles_shape, rows_shape, rows_shape),
                [wanted, asked, returned, *others],
                2**16,
                2**22,
                [pltpu.VMEM((3, 8 * NLEAF, LEAF), F32), pltpu.VMEM((8 * NLEAF, LEAF), F32)],
            )

        return run

    *placed, wanted = call(
        request_kernel,
        (ends_shape, ends_shape, shape(DEVICES, LEAF, dtype=jnp.int32)),
        [pair_owner.transpose(0, 2, 1), pair_slot.transpose(0, 2, 1), bins],
        2**26,
        2**18,
        [
            pltpu.VMEM((2, 2, PAIRS), jnp.int32),
            pltpu.VMEM((2, 2, PAIRS), jnp.int32),
            pltpu.VMEM((NLEAF, LEAF), jnp.int32),
            dma((3,)),
        ],
        [pl.BlockSpec(memory_space=pltpu.HBM)] * 3,
        vmem=60 * 2**20,
    )
    wanted = exchange(wanted.reshape(DEVICES, 1, LEAF)).reshape(DEVICES, LEAF)
    state, where, moving, *placed, order, ordered = call(
        pack_kernel,
        (
            tiles_shape, rows_shape, rows_shape, ends_shape, ends_shape,
            shape(NLEAF, LEAF, dtype=jnp.int32), tiles_shape,
        ),
        [positions, velocities, masses, bins, *placed],
        2**16,
        2**20,
        [pltpu.VMEM((2, 8 * NLEAF, LEAF), F32)],
    )
    looked, asked, most = call(
        gather_kernel,
        (looked_shape, shape(2 * CAP, DEVICES, dtype=jnp.int32), shape(1, 1, dtype=jnp.int32)),
        [wanted, ordered],
        2**16,
        2**21,
    )
    local = local_forces(local_ids[0], state)
    few = most[0, 0] <= LEAF // 2
    looked, state, where, moving = lax.cond(
        few, subcycle0(True), subcycle0(False),
        placed[0], send_leaves(looked), wanted, asked, local, masses, where, moving, bins, order,
    )
    local = local_forces(local_ids[1], state)
    pushed = remote_forces(placed[1], send_leaves(looked), local)
    returned = send_forces(pushed)
    out = shape(3, NLEAF * LEAF)
    return call(
        finish_kernel,
        (out, out, out),
        [asked, returned, local, where, moving, bins],
        2**16,
        2**22,
        [
            pltpu.VMEM((3, 8 * NLEAF, LEAF), F32),
            *[pltpu.VMEM((3, NLEAF * LEAF), F32)] * 3,
            dma((3,)),
        ],
        out_specs=(anywhere,) * 3,
    )


def solution(mesh):
    split = P(None, AXES)
    rows = P(None, AXES, None)
    return jax.shard_map(
        shards,
        mesh=mesh,
        in_specs=(split, split, P(AXES), P(AXES), rows, rows, rows),
        out_specs=(split, split, split),
        check_vma=False,
    )
```
